512 devices in a mesh: expert: 64 (over x, z, core), dp: 8 (over y).
Axes of the slice: x: 4, y: 8, z: 8, core: 2. Of those that a mesh axis runs over, the one named last changes fastest.
Arguments:
- tokens: bfloat16 [16384, 6144], P('expert', 'dp'), may hold values from -6 to 6
- grad_out: bfloat16 [16384, 6144], P('expert', 'dp'), may hold values from -0.625 to 0.625
- combine: bfloat16 [16384, 2], P('expert'), may hold values from 0.049804688 to 1
- routes: int32 [16384, 2], P('expert'), may hold values from 0 to 63, all different within a row; in each aligned block of 256 rows (0 to 255, 256 to 511, ...) at most 9 rows name the same one
- w_gate: bfloat16 [64, 256, 6144], P('expert', None, 'dp'), may hold values from -0.078125 to 0.078125
- w_up: bfloat16 [64, 256, 6144], P('expert', None, 'dp'), may hold values from -0.078125 to 0.078125
- w_down: bfloat16 [64, 256, 6144], P('expert', None, 'dp'), may hold values from -0.375 to 0.375
Outputs:
- grad_gate: bfloat16 [64, 256, 6144], P('expert', None, 'dp')
- grad_up: bfloat16 [64, 256, 6144], P('expert', None, 'dp')
- grad_down: bfloat16 [64, 256, 6144], P('expert', None, 'dp')
- grad_combine: float32 [16384, 2], P('expert')
The draws below stay inside these ranges and needn't reach their ends.
Inputs may be any that keep to these rules, and one draw needn't show every extreme that they name: `routes`: each token names 2 different experts. Among the tokens of one index of the expert axis no expert is named by more than 9 tokens, and on some index one expert is named by exactly 9 tokens.
All inputs are finite; a program needn't handle non-finite values.
Results may differ from the reference program's by a relative error of at most 0.0049.
Values may be sent and summed in bfloat16 or wider, within the bound.
No kernel may reach another device: no remote copies, remote signals or barrier semaphores. Data moves between devices by JAX's collectives and lax.ppermute only.
A program may use at most 64 MiB of HBM per device.

```python
import math
import jax
import jax.numpy as jnp
import numpy as np
from jax import lax

D = 6144
FH = 256
TOP = 2
TOK = 256
EXPERTS = 64
TOKENS = 16384
MOST = 9
N_EXPERT = 64


def level_of(key, extent, shards, smallest, high):
    gain = 1.0
    for dim, parts in shards:
        heights = jax.random.uniform(jax.random.fold_in(jax.random.fold_in(key, 6), dim), (parts,), jnp.float32, smallest / len(shards), high / len(shards))
        gain = gain * jnp.repeat(jnp.exp(heights), extent[dim] // parts).reshape((-1,) + (1,) * (len(extent) - 1 - dim))
    return gain


def assign_block(own_key, own, number, rows, amount, top, most, lean):
    order = jax.random.permutation(own_key, amount)
    packed, ordinary = load_shares(amount, rows * top, most, lean, True), load_shares(amount, rows * top, most, lean, False)
    places = jnp.arange(amount)

    def named(sizes, offset_by):
        used = int((sizes > 0).sum())
        fixed = max(1, used // 4)
        shifted = fixed + (places - fixed + offset_by * (used - fixed)) % max(1, amount - fixed)
        return jnp.zeros((amount,), jnp.int32).at[order[jnp.where(places < fixed, places, shifted)]].set(jnp.asarray(sizes, jnp.int32))

    sizes = jnp.where(number % 4 == 0, named(packed, number // 4), named(ordinary, number - number // 4 - 1))
    mixed = jax.random.permutation(jax.random.fold_in(own, 3), amount)
    donor, sink = mixed[0:amount // 2 * 2:2], mixed[1:amount // 2 * 2:2]
    slack = jnp.minimum(sizes[donor] - 1, most - sizes[sink]) // 2
    slack = jnp.where((donor == order[0]) | (sink == order[0]) | (sizes[sink] == 0), 0, jnp.maximum(slack, 0))
    shifted = jax.random.randint(jax.random.fold_in(own, 4), (amount // 2,), 0, 1 << 20) % (slack + 1)
    sizes = sizes.at[donor].add(-shifted).at[sink].add(shifted)
    items = jnp.searchsorted(jnp.cumsum(sizes), jnp.arange(rows * top), side="right").astype(jnp.int32)
    grid = items.reshape(top, rows).T
    grid = grid[jax.random.permutation(jax.random.fold_in(own, 1), rows)]
    offset_by = jax.random.randint(jax.random.fold_in(own, 2), (rows, 1), 0, top)
    return jnp.take_along_axis(grid, (jnp.arange(top)[None, :] + offset_by) % top, axis=1)


def load_shares(count, total, bound, lean, full):
    portions = [(1 << 20) // math.isqrt(grade ** lean) + 1 for grade in range(1, count + 1)]
    largest = bound if full else min(bound, max(-(-total // count), total * portions[0] // sum(portions)))
    least = 1 if total - largest >= count - 1 else 0
    given, surplus = [largest] + [least] * (count - 1), total - largest - least * (count - 1)
    while surplus > 0:
        movable = [i for i in range(1, count) if given[i] < largest] or [i for i in range(1, count) if given[i] < bound]
        whole, left = sum([portions[i] for i in movable]), surplus
        for i in movable:
            extra = min(bound - given[i], max(1, left * portions[i] // whole), surplus)
            given[i] = given[i] + extra
            surplus = surplus - extra
    return np.array(given)


def normal_values(rng, shape, scale, bound, split=(), kind=jnp.bfloat16):
    gain = level_of(rng, shape, split, -0.22, 0.18) if split else 1.0
    array = jax.random.normal(rng, shape, jnp.float32) * scale * gain
    return jnp.minimum(jnp.maximum(array, -bound), bound).astype(kind)


def setup_inputs(seed: int = 0) -> dict:
    arg_keys = jax.random.split(jax.random.key(seed), 8)
    tokens = normal_values(arg_keys[0], (TOKENS, D), 1.0, 6.0, ((0, 64), (1, 8)))
    grad_out = normal_values(arg_keys[1], (TOKENS, D), ((TOK * TOP) ** -0.5), 0.625, ((0, 64), (1, 8)))
    combine = jnp.clip(0.049804688 + 0.9501953 * jax.random.uniform(arg_keys[2], (TOKENS, TOP), jnp.float32) ** level_of(arg_keys[2], (TOKENS, TOP), ((0, 64),), -0.2, 0.2), 0.049804688, 1.0).astype(jnp.bfloat16)
    routes_keys = jax.random.split(jax.random.fold_in(arg_keys[3], 1), TOKENS // TOK)
    routes_turns = jax.random.permutation(jax.random.fold_in(arg_keys[3], 3), TOKENS // TOK)
    routes = jax.vmap(lambda own, number: assign_block(jax.random.fold_in(arg_keys[3], 2), own, number, TOK, EXPERTS, TOP, MOST, 2))(routes_keys, routes_turns).reshape((TOKENS, TOP))
    w_gate = normal_values(arg_keys[4], (EXPERTS, FH, D), D ** -0.5, 0.078125, ((0, 64), (2, 8)))
    w_up = normal_values(arg_keys[5], (EXPERTS, FH, D), D ** -0.5, 0.078125, ((0, 64), (2, 8)))
    w_down = normal_values(arg_keys[6], (EXPERTS, FH, D), FH ** -0.5, 0.375, ((0, 64), (2, 8)))
    return {"tokens": tokens, "grad_out": grad_out, "combine": combine, "routes": routes, "w_gate": w_gate, "w_up": w_up, "w_down": w_down}


inner_dims = (((1,), (1,)), ((), ()))
outer_dims = (((0,), (0,)), ((), ()))


def silu_parts(gate_pre):
    sig_val = jax.nn.sigmoid(gate_pre)
    return gate_pre * sig_val, sig_val * (1.0 + gate_pre * (1.0 - sig_val))


def reference(tokens, grad_out, combine, routes, w_gate, w_up, w_down):
    assigned = TOKENS * TOP
    expert_cap = MOST * N_EXPERT
    flat_expert = routes.reshape(-1).astype(jnp.int32)
    token_of = (jnp.arange(assigned, dtype=jnp.int32) // TOP).astype(jnp.int32)
    flat_prob = combine.reshape(-1)
    ordering = jnp.argsort(flat_expert, stable=True).astype(jnp.int32)
    counts = jnp.zeros((EXPERTS,), jnp.int32).at[flat_expert].add(1)
    starts = (jnp.cumsum(counts) - counts).astype(jnp.int32)
    padded = jnp.concatenate([ordering, jnp.zeros((expert_cap,), jnp.int32)])

    def one_expert(expert):
        picked = lax.dynamic_slice(padded, (starts[expert],), (expert_cap,))
        valid = jnp.arange(expert_cap, dtype=jnp.int32) < counts[expert]
        rows_tok = token_of[picked]
        rows_x = tokens[rows_tok]
        rows_dy = grad_out[rows_tok]
        weight = jnp.where(valid, flat_prob[picked].astype(jnp.float32), jnp.float32(0.0))[:, None]
        gate_pre = lax.dot_general(rows_x, w_gate[expert], inner_dims, preferred_element_type=jnp.float32)
        up_pre = lax.dot_general(rows_x, w_up[expert], inner_dims, preferred_element_type=jnp.float32)
        grad_hid = lax.dot_general(rows_dy, w_down[expert], inner_dims, preferred_element_type=jnp.float32)
        silu_out, silu_slope = silu_parts(gate_pre)
        hidden = silu_out * up_pre
        weighted = (weight * hidden).astype(jnp.bfloat16)
        scaled = weight * grad_hid
        up_rows = (scaled * silu_out).astype(jnp.bfloat16)
        gate_rows = (scaled * up_pre * silu_slope).astype(jnp.bfloat16)
        scores = jnp.sum(hidden * grad_hid, axis=1)
        gate_grad = lax.dot_general(gate_rows, rows_x, outer_dims, preferred_element_type=jnp.float32)
        up_grad = lax.dot_general(up_rows, rows_x, outer_dims, preferred_element_type=jnp.float32)
        down_grad = lax.dot_general(weighted, rows_dy, outer_dims, preferred_element_type=jnp.float32)
        target = jnp.where(valid, picked, assigned).astype(jnp.int32)
        return gate_grad, up_grad, down_grad, scores, target

    gate_all, up_all, down_all, score_all, target_all = lax.map(one_expert, jnp.arange(EXPERTS, dtype=jnp.int32))
    grad_combine = jnp.zeros((assigned + 1,), jnp.float32).at[target_all.reshape(-1)].set(score_all.reshape(-1))
    grad_combine = grad_combine[:assigned].reshape(TOKENS, TOP)
    return (gate_all.astype(jnp.bfloat16), up_all.astype(jnp.bfloat16), down_all.astype(jnp.bfloat16), grad_combine)
```

```python
import functools

import jax
import jax.numpy as jnp
from jax import lax
from jax.experimental import pallas as pl
from jax.experimental.pallas import tpu as pltpu
from jax.sharding import PartitionSpec as P

bf16, f32, i32 = jnp.bfloat16, jnp.float32, jnp.int32
LANES, SUB = 128, 8
CAP = 9
LIMIT = 32 * 2**20


def params():
    return pltpu.CompilerParams(vmem_limit_bytes=LIMIT)


def iota(shape, dim):
    return lax.broadcasted_iota(i32, shape, dim)


def mm(a, b, contract=((1,), (0,))):
    return lax.dot_general(a, b, (contract, ((), ())), preferred_element_type=f32)


def pack_kernel(routes, combine, tokens, grads, out, ranks):
    experts, toks = ranks.shape
    blocks = tokens.shape[1] // LANES
    e = iota((experts, toks), 0)
    first, second = e == routes[0:1, :], e == routes[1:2, :]
    named = first | second
    hot = jnp.where(named, 1.0, 0.0).astype(bf16)
    before = jnp.where(iota((toks, toks), 0) < iota((toks, toks), 1), 1.0, 0.0).astype(bf16)
    rank = jnp.where(named, mm(hot, before), -1.0)
    ranks[...] = rank
    prob = combine[...].astype(f32)
    prob = jnp.where(first, prob[0:1, :], jnp.where(second, prob[1:2, :], 0.0))

    slot = iota((experts, SUB, toks), 1)
    spread = jnp.broadcast_to(rank[:, None, :], (experts, SUB, toks))
    pick = jnp.where(spread == slot.astype(f32), 1.0, 0.0)
    pick = pick.reshape(experts * SUB, toks).astype(bf16)
    for i, source in enumerate((tokens, grads)):
        rows = mm(pick, source[...])
        for c in range(blocks):
            tile = rows[:, c * LANES : (c + 1) * LANES].reshape(experts, SUB, LANES)
            at = (i * blocks + c) * SUB
            out[:, at : at + SUB, :] = tile.astype(bf16)

    ninth = jnp.where(rank == float(SUB), 1.0, 0.0)
    ninth = jnp.broadcast_to(ninth[:, None, :], (experts, SUB, toks))
    places = [(tokens, c) for c in range(blocks)] + [(grads, c) for c in range(blocks)]
    at = 2 * blocks * SUB
    for base in range(0, len(places) + 1, SUB):
        total = jnp.zeros((experts * SUB, LANES), f32)
        for k, (source, c) in enumerate(places[base : base + SUB]):
            mask = jnp.where(slot == k, ninth, 0.0).reshape(experts * SUB, toks).astype(bf16)
            total = total + mm(mask, source[:, c * LANES : (c + 1) * LANES])
        total = total.reshape(experts, SUB, LANES)
        if base + SUB > len(places):
            lane = iota((experts, LANES), 1)
            row = jnp.zeros((experts, LANES), f32)
            for r in range(CAP):
                value = jnp.sum(jnp.where(rank == float(r), prob, 0.0), axis=1, keepdims=True)
                row = jnp.where(lane == r, value, row)
            row = jnp.broadcast_to(row[:, None, :], (experts, SUB, LANES))
            total = jnp.where(iota((experts, SUB, LANES), 1) == len(places) - base, row, total)
        out[:, at + base : at + base + SUB, :] = total.astype(bf16)


def pack(routes, combine, tokens, grads, experts):
    toks, width = tokens.shape
    rows = (2 * width // LANES) * SUB + 2 * SUB
    return pl.pallas_call(
        pack_kernel,
        out_shape=(
            jax.ShapeDtypeStruct((experts, rows, LANES), bf16),
            jax.ShapeDtypeStruct((experts, toks), f32),
        ),
        compiler_params=params(),
        name="pack",
    )(routes, combine, tokens, grads)


def project_kernel(me, recv, w_gate, w_up, w_down, part, own, rows_x, rows_dy, probs):
    experts = recv.shape[0]
    groups, count, _ = part.shape
    width = rows_x.shape[1]
    blocks = width // LANES
    main = experts * SUB
    share = main // groups

    def tile(at):
        return recv[:, at : at + SUB, :].astype(f32).reshape(main, LANES).astype(bf16)

    at = 2 * blocks * SUB
    last = [tile(at), tile(at + SUB)]
    column, line = iota((experts, main), 1), iota((experts, main), 0)

    def taken(index):
        pick = jnp.where(column == line * SUB + index % SUB, 1.0, 0.0).astype(bf16)
        return mm(pick, last[index // SUB])

    for i, rows in enumerate((rows_x, rows_dy)):
        for c in range(blocks):
            lanes = slice(c * LANES, (c + 1) * LANES)
            rows[0:main, lanes] = tile((i * blocks + c) * SUB)
            rows[main:, lanes] = taken(i * blocks + c).astype(bf16)
    probs[...] = taken(2 * blocks)

    x, dy = rows_x[...], rows_dy[...]
    hidden = w_gate.shape[1]
    for i, (rows, weight) in enumerate(((x, w_gate), (x, w_up), (dy, w_down))):
        lanes = slice(i * hidden, (i + 1) * hidden)
        value = mm(rows, weight[0], ((1,), (1,)))
        for j in range(groups):
            piece = jnp.concatenate(
                [value[j * share : (j + 1) * share], value[main + j * SUB : main + (j + 1) * SUB]]
            )
            part[j, :, lanes] = piece.astype(bf16)

            @pl.when(me[0] == j)
            def _(piece=piece, lanes=lanes):
                own[:, lanes] = piece


def project(me, recv, w_gate, w_up, w_down, groups):
    experts = recv.shape[0]
    hidden, width = w_gate.shape[1:]
    total = experts * CAP
    count = total // groups
    vmem = pl.BlockSpec(memory_space=pltpu.VMEM)
    return pl.pallas_call(
        project_kernel,
        in_specs=[pl.BlockSpec(memory_space=pltpu.SMEM)] + [vmem] * 4,
        out_shape=(
            jax.ShapeDtypeStruct((groups, count, 3 * hidden), bf16),
            jax.ShapeDtypeStruct((count, 3 * hidden), f32),
            jax.ShapeDtypeStruct((total, width), bf16),
            jax.ShapeDtypeStruct((total, width), bf16),
            jax.ShapeDtypeStruct((experts, LANES), f32),
        ),
        compiler_params=params(),
        name="project",
    )(me, recv, w_gate, w_up, w_down)


def terms_kernel(me, parts, own, probs, out):
    groups, count, _ = parts.shape
    hidden = parts.shape[2] // 3
    main = count - SUB
    near = probs[pl.ds(pl.multiple_of(me[0] * SUB, SUB), SUB), :]
    lane = iota((SUB, SUB, LANES), 2)
    spread = jnp.broadcast_to(near[:, None, :], (SUB, SUB, LANES))
    picked = jnp.sum(jnp.where(lane == iota((SUB, SUB, LANES), 1), spread, 0.0), axis=2, keepdims=True)
    ninth = jnp.sum(jnp.where(iota((SUB, LANES), 1) == SUB, near, 0.0), axis=1, keepdims=True)
    weight = jnp.concatenate([picked.reshape(main, 1), ninth])

    def total(i):
        lanes = slice(i * hidden, (i + 1) * hidden)
        value = own[:, lanes]
        for j in range(groups):
            value = value + jnp.where(me[0] == j, 0.0, parts[j, :, lanes].astype(f32))
        return value

    gate_pre, up_pre, grad_hid = total(0), total(1), total(2)
    sig = jax.nn.sigmoid(gate_pre)
    silu_out = gate_pre * sig
    inner = silu_out * up_pre
    scaled = weight * grad_hid
    out[:, 0:hidden] = (scaled * up_pre * (sig * (1.0 + gate_pre * (1.0 - sig)))).astype(bf16)
    out[:, hidden : 2 * hidden] = (scaled * silu_out).astype(bf16)
    out[:, 2 * hidden : 3 * hidden] = (weight * inner).astype(bf16)
    score = jnp.sum(inner * grad_hid, axis=1, keepdims=True)
    high = score.astype(bf16).astype(f32)
    middle = (score - high).astype(bf16).astype(f32)
    low = score - high - middle
    lane = iota((count, LANES), 1)
    triple = jnp.where(lane == 0, high, jnp.where(lane == 1, middle, jnp.where(lane == 2, low, 0.0)))
    out[:, 3 * hidden :] = triple.astype(bf16)


def terms(me, parts, own, probs):
    count, wide = own.shape
    vmem = pl.BlockSpec(memory_space=pltpu.VMEM)
    return pl.pallas_call(
        terms_kernel,
        in_specs=[pl.BlockSpec(memory_space=pltpu.SMEM)] + [vmem] * 3,
        out_shape=jax.ShapeDtypeStruct((count, wide + LANES), bf16),
        compiler_params=params(),
        name="terms",
    )(me, parts, own, probs)


def scores_kernel(triples, out):
    groups, count, _ = triples.shape
    main = count - SUB
    score = jnp.sum(triples[...].astype(f32), axis=2, keepdims=True)
    sources = groups * SUB
    lane, slot = iota((sources, SUB, LANES), 2), iota((sources, SUB, LANES), 1)
    direct = jnp.broadcast_to(score[:, :main].reshape(sources, SUB, 1), (sources, SUB, LANES))
    ninth = jnp.broadcast_to(score[:, main:], (groups, SUB, LANES))
    ninth = jnp.broadcast_to(ninth[:, None], (groups, SUB, SUB, LANES)).reshape(sources, SUB, LANES)
    mine = lax.rem(iota((sources, SUB, LANES), 0), SUB) == slot
    both = jnp.where(lane == slot, direct, jnp.where((lane == SUB) & mine, ninth, 0.0))
    out[...] = jnp.sum(both, axis=1, keepdims=True)


def scores_by_source(triples, sources):
    return pl.pallas_call(
        scores_kernel,
        out_shape=jax.ShapeDtypeStruct((sources, 1, LANES), f32),
        compiler_params=params(),
        name="scores",
    )(triples)


def outer_kernel(rows, rows_x, rows_dy, gate, up, down):
    groups, count, _ = rows.shape
    hidden = gate.shape[1]
    main = count - SUB
    x, dy = rows_x[...], rows_dy[...]
    for i, (other, out) in enumerate(((x, gate), (x, up), (dy, down))):
        lanes = slice(i * hidden, (i + 1) * hidden)
        direct = rows[:, 0:main, lanes].astype(f32).reshape(groups * main, hidden)
        ninth = rows[:, main:, lanes].astype(f32).reshape(groups * SUB, hidden)
        value = jnp.concatenate([direct, ninth]).astype(bf16)
        out[0] = mm(value, other, ((0,), (0,))).astype(bf16)


def outer(rows, rows_x, rows_dy, hidden):
    total, width = rows_x.shape
    return pl.pallas_call(
        outer_kernel,
        out_shape=(jax.ShapeDtypeStruct((1, hidden, width), bf16),) * 3,
        compiler_params=params(),
        cost_estimate=pl.CostEstimate(
            flops=6 * total * width * hidden, bytes_accessed=8 * total * width, transcendentals=0
        ),
        name="outer",
    )(rows, rows_x, rows_dy)


def place_kernel(routes, ranks, scores, out):
    experts, toks = ranks.shape
    spread = jnp.broadcast_to(scores[...], (experts, SUB, LANES))
    spread = spread.reshape(experts // SUB, SUB, SUB, LANES)
    mine = iota(spread.shape, 1) == iota(spread.shape, 2)
    table = jnp.sum(jnp.where(mine, spread, 0.0), axis=1).reshape(experts, LANES)
    rank = ranks[...]
    value = jnp.zeros((experts, toks), f32)
    for r in range(CAP):
        value = jnp.where(rank == float(r), table[:, r : r + 1], value)
    e = iota((experts, toks), 0)
    for k in range(2):
        out[k : k + 1, :] = jnp.sum(
            jnp.where(e == routes[k : k + 1, :], value, 0.0), axis=0, keepdims=True
        )


def place(routes, ranks, scores):
    return pl.pallas_call(
        place_kernel,
        out_shape=jax.ShapeDtypeStruct(routes.shape, f32),
        compiler_params=params(),
        name="place",
    )(routes, ranks, scores)


def local(tokens, grad_out, combine, routes, w_gate, w_up, w_down):
    experts, groups = lax.axis_size("expert"), lax.axis_size("dp")
    hidden = w_gate.shape[1]
    me = lax.axis_index("dp").astype(i32).reshape(1)
    by_slot = routes.T
    packed, ranks = pack(by_slot, combine.T, tokens, grad_out, experts)
    recv = lax.all_to_all(packed, "expert", split_axis=0, concat_axis=0, tiled=True)
    part, own, rows_x, rows_dy, probs = project(me, recv, w_gate, w_up, w_down, groups)
    parts = lax.all_to_all(part, "dp", split_axis=0, concat_axis=0, tiled=True)
    mine = terms(me, parts, own, probs)
    rows = lax.all_gather(mine, "dp", axis=0, tiled=False)
    triples = rows[:, :, 3 * hidden :]
    returned = lax.all_to_all(
        scores_by_source(triples, experts), "expert", split_axis=0, concat_axis=0, tiled=True
    )
    grads = outer(rows, rows_x, rows_dy, hidden)
    return tuple(grads) + (place(by_slot, ranks, returned).T,)


def solution(mesh):
    placed = (
        P("expert", "dp"),
        P("expert", "dp"),
        P("expert", None),
        P("expert", None),
        P("expert", None, "dp"),
        P("expert", None, "dp"),
        P("expert", None, "dp"),
    )
    return jax.shard_map(
        local,
        mesh=mesh,
        in_specs=placed,
        out_specs=(
            P("expert", None, "dp"),
            P("expert", None, "dp"),
            P("expert", None, "dp"),
            P("expert", None),
        ),
        check_vma=False,
    )
```

```python
import functools

import jax
import jax.numpy as jnp
from jax import lax
from jax.experimental import pallas as pl
from jax.experimental.pallas import tpu as pltpu
from jax.sharding import PartitionSpec as P

bf16, f32, i32 = jnp.bfloat16, jnp.float32, jnp.int32
LANES, SUB = 128, 8
CAP = 9
LIMIT = 32 * 2**20
WHOLE = 64 * 2**20 - 2**19


def params(limit=LIMIT):
    return pltpu.CompilerParams(vmem_limit_bytes=limit)


def iota(shape, dim):
    return lax.broadcasted_iota(i32, shape, dim)


def mm(a, b, contract=((1,), (0,))):
    return lax.dot_general(a, b, (contract, ((), ())), preferred_element_type=f32)


def copies(pairs, sems):
    return [pltpu.make_async_copy(src, dst, sems.at[i]) for i, (src, dst) in enumerate(pairs)]


def rank_of(routes, experts, toks):
    e = iota((experts, toks), 0)
    first, second = e == routes[0:1, :], e == routes[1:2, :]
    named = first | second
    hot = jnp.where(named, 1.0, 0.0).astype(bf16)
    before = jnp.where(iota((toks, toks), 0) < iota((toks, toks), 1), 1.0, 0.0).astype(bf16)
    return first, second, jnp.where(named, mm(hot, before), -1.0)


def pack_kernel(routes_h, combine_h, tokens_h, grads_h, out_h, routes, combine, tokens, grads, out, last, ins, outs):
    experts = out.shape[0]
    toks, width = tokens.shape
    blocks = width // LANES
    half = blocks * SUB
    arriving = copies(
        [(routes_h, routes), (combine_h, combine), (tokens_h, tokens), (grads_h, grads)], ins
    )
    for c in arriving:
        c.start()
    arriving[0].wait()
    first, second, rank = rank_of(routes, experts, toks)
    slot = iota((experts, SUB, toks), 1)
    spread = jnp.broadcast_to(rank[:, None, :], (experts, SUB, toks))
    pick = jnp.where(spread == slot.astype(f32), 1.0, 0.0)
    pick = pick.reshape(experts * SUB, toks).astype(bf16)
    ninth = jnp.where(rank == float(SUB), 1.0, 0.0).astype(bf16)
    pieces = [slice(0, half), slice(half, 2 * half), slice(2 * half, 2 * half + 2 * SUB)]
    leaving = copies([(out.at[:, p], out_h.at[:, p]) for p in pieces], outs)
    last[...] = jnp.zeros(last.shape, f32)
    for i, source in enumerate((tokens, grads)):
        arriving[2 + i].wait()
        rows = mm(pick, source[...])
        for c in range(blocks):
            tile = rows[:, c * LANES : (c + 1) * LANES].reshape(experts, SUB, LANES)
            at = i * half + c * SUB
            out[:, at : at + SUB, :] = tile.astype(bf16)
        leaving[i].start()
        rows = mm(ninth, source[...])
        for c in range(blocks):
            place = i * blocks + c
            last[place // SUB, pl.ds(place % SUB, experts, stride=SUB), :] = rows[:, c * LANES : (c + 1) * LANES]
    arriving[1].wait()
    prob = combine[...].astype(f32)
    prob = jnp.where(first, prob[0:1, :], jnp.where(second, prob[1:2, :], 0.0))
    lane = iota((experts, LANES), 1)
    row = jnp.zeros((experts, LANES), f32)
    for r in range(CAP):
        value = jnp.sum(jnp.where(rank == float(r), prob, 0.0), axis=1, keepdims=True)
        row = jnp.where(lane == r, value, row)
    place = 2 * blocks
    last[place // SUB, pl.ds(place % SUB, experts, stride=SUB), :] = row
    for k in range(2):
        at = 2 * half + k * SUB
        out[:, at : at + SUB, :] = last[k].reshape(experts, SUB, LANES).astype(bf16)
    leaving[2].start()
    for c in leaving:
        c.wait()


def pack(routes, combine, tokens, grads, experts):
    toks, width = tokens.shape
    shape = (experts, (2 * width // LANES) * SUB + 2 * SUB, LANES)
    args = (routes, combine, tokens, grads)
    return pl.pallas_call(
        pack_kernel,
        in_specs=[pl.BlockSpec(memory_space=pltpu.HBM)] * 4,
        out_specs=pl.BlockSpec(memory_space=pltpu.HBM),
        out_shape=jax.ShapeDtypeStruct(shape, bf16),
        scratch_shapes=[pltpu.VMEM(a.shape, a.dtype) for a in args]
        + [
            pltpu.VMEM(shape, bf16),
            pltpu.VMEM((2, experts * SUB, LANES), f32),
            pltpu.SemaphoreType.DMA((4,)),
            pltpu.SemaphoreType.DMA((3,)),
        ],
        compiler_params=params(WHOLE),
        name="pack",
    )(*args)


def stage_kernel(gate, up, down, out):
    for i, weight in enumerate((gate, up, down)):
        out[i] = weight[0].astype(f32).T.astype(bf16)


def stage(*weights):
    _, hidden, width = weights[0].shape
    return pl.pallas_call(
        stage_kernel,
        out_shape=jax.ShapeDtypeStruct((len(weights), width, hidden), bf16),
        compiler_params=params(),
        cost_estimate=pl.CostEstimate(
            flops=3 * width * hidden, bytes_accessed=12 * width * hidden, transcendentals=0
        ),
        name="stage",
    )(*weights)


def project_kernel(me, recv, weights, part, own, rows_x, rows_dy, probs, last):
    experts = recv.shape[0]
    groups, count, _ = part.shape
    _, width, hidden = weights.shape
    blocks = width // LANES
    main = experts * SUB
    share = main // groups

    def tile(at):
        return recv[:, at : at + SUB, :].astype(f32).reshape(main, LANES)

    for k in range(2):
        last[k] = tile((2 * blocks + k) * SUB)

    def taken(place):
        return last[place // SUB, pl.ds(place % SUB, experts, stride=SUB), :]

    probs[...] = taken(2 * blocks)
    for i, rows in enumerate((rows_x, rows_dy)):
        for c in range(blocks):
            lanes = slice(c * LANES, (c + 1) * LANES)
            rows[0:main, lanes] = tile((i * blocks + c) * SUB).astype(bf16)
            rows[main:, lanes] = taken(i * blocks + c).astype(bf16)
    for i, rows in enumerate((rows_x, rows_x, rows_dy)):
        lanes = slice(i * hidden, (i + 1) * hidden)
        value = mm(rows[...], weights[i])
        for j in range(groups):
            piece = jnp.concatenate(
                [value[j * share : (j + 1) * share], value[main + j * SUB : main + (j + 1) * SUB]]
            )
            part[j, :, lanes] = piece.astype(bf16)

            @pl.when(me[0] == j)
            def _(piece=piece, lanes=lanes):
                own[:, lanes] = piece


def project(me, recv, weights, groups):
    experts = recv.shape[0]
    _, width, hidden = weights.shape
    total = experts * CAP
    count = total // groups
    vmem = pl.BlockSpec(memory_space=pltpu.VMEM)
    return pl.pallas_call(
        project_kernel,
        in_specs=[pl.BlockSpec(memory_space=pltpu.SMEM)] + [vmem] * 2,
        out_shape=(
            jax.ShapeDtypeStruct((groups, count, 3 * hidden), bf16),
            jax.ShapeDtypeStruct((count, 3 * hidden), f32),
            jax.ShapeDtypeStruct((total, width), bf16),
            jax.ShapeDtypeStruct((total, width), bf16),
            jax.ShapeDtypeStruct((experts, LANES), f32),
        ),
        scratch_shapes=[pltpu.VMEM((2, experts * SUB, LANES), f32)],
        compiler_params=params(),
        name="project",
    )(me, recv, weights)


def terms_kernel(me, parts, own, probs, out):
    groups, count, _ = parts.shape
    hidden = parts.shape[2] // 3
    main = count - SUB
    near = probs[pl.ds(pl.multiple_of(me[0] * SUB, SUB), SUB), :]
    lane = iota((SUB, SUB, LANES), 2)
    spread = jnp.broadcast_to(near[:, None, :], (SUB, SUB, LANES))
    picked = jnp.sum(jnp.where(lane == iota((SUB, SUB, LANES), 1), spread, 0.0), axis=2, keepdims=True)
    ninth = jnp.sum(jnp.where(iota((SUB, LANES), 1) == SUB, near, 0.0), axis=1, keepdims=True)
    weight = jnp.concatenate([picked.reshape(main, 1), ninth])

    def total(i):
        lanes = slice(i * hidden, (i + 1) * hidden)
        value = own[:, lanes]
        for j in range(groups):
            value = value + jnp.where(me[0] == j, 0.0, parts[j, :, lanes].astype(f32))
        return value

    gate_pre, up_pre, grad_hid = total(0), total(1), total(2)
    sig = jax.nn.sigmoid(gate_pre)
    silu_out = gate_pre * sig
    inner = silu_out * up_pre
    scaled = weight * grad_hid
    out[:, 0:hidden] = (scaled * up_pre * (sig * (1.0 + gate_pre * (1.0 - sig)))).astype(bf16)
    out[:, hidden : 2 * hidden] = (scaled * silu_out).astype(bf16)
    out[:, 2 * hidden : 3 * hidden] = (weight * inner).astype(bf16)
    score = jnp.sum(inner * grad_hid, axis=1, keepdims=True)
    cube = (SUB, SUB, LANES)
    direct = jnp.broadcast_to(score[:main].reshape(SUB, SUB, 1), cube)
    table = jnp.sum(jnp.where(iota(cube, 2) == iota(cube, 1), direct, 0.0), axis=1)
    table = jnp.where(iota((SUB, LANES), 1) == SUB, score[main:], table)
    high = table.astype(bf16).astype(f32)
    middle = (table - high).astype(bf16).astype(f32)
    low = table - high - middle
    rest = jnp.zeros((count - 3 * SUB, LANES), f32)
    out[:, 3 * hidden :] = jnp.concatenate([high, middle, low, rest]).astype(bf16)


def terms(me, parts, own, probs):
    count, wide = own.shape
    vmem = pl.BlockSpec(memory_space=pltpu.VMEM)
    return pl.pallas_call(
        terms_kernel,
        in_specs=[pl.BlockSpec(memory_space=pltpu.SMEM)] + [vmem] * 3,
        out_shape=jax.ShapeDtypeStruct((count, wide + LANES), bf16),
        compiler_params=params(),
        name="terms",
    )(me, parts, own, probs)


def outer_kernel(routes, rows, rows_x, rows_dy, gate, up, down, ranks):
    groups, count, _ = rows.shape
    hidden = gate.shape[1]
    main = count - SUB
    x, dy = rows_x[...], rows_dy[...]
    for i, (other, out) in enumerate(((x, gate), (x, up), (dy, down))):
        lanes = slice(i * hidden, (i + 1) * hidden)
        direct = rows[:, 0:main, lanes].astype(f32).reshape(groups * main, hidden)
        ninth = rows[:, main:, lanes].astype(f32).reshape(groups * SUB, hidden)
        value = jnp.concatenate([direct, ninth]).astype(bf16)
        out[0] = mm(value, other, ((0,), (0,))).astype(bf16)
    ranks[...] = rank_of(routes, *ranks.shape)[2]


def outer(routes, rows, rows_x, rows_dy, hidden, experts):
    total, width = rows_x.shape
    return pl.pallas_call(
        outer_kernel,
        out_shape=(jax.ShapeDtypeStruct((1, hidden, width), bf16),) * 3
        + (jax.ShapeDtypeStruct((experts, routes.shape[1]), f32),),
        compiler_params=params(),
        cost_estimate=pl.CostEstimate(
            flops=6 * total * width * hidden, bytes_accessed=8 * total * width, transcendentals=0
        ),
        name="outer",
    )(routes, rows, rows_x, rows_dy)


def place_kernel(routes, ranks, scores, out):
    experts, toks = ranks.shape
    rank = ranks[...]
    value = jnp.zeros((experts, toks), f32)
    for r in range(CAP):
        value = jnp.where(rank == float(r), scores[:, r : r + 1], value)
    e = iota((experts, toks), 0)
    for k in range(2):
        out[k : k + 1, :] = jnp.sum(
            jnp.where(e == routes[k : k + 1, :], value, 0.0), axis=0, keepdims=True
        )


def place(routes, ranks, scores):
    return pl.pallas_call(
        place_kernel,
        out_shape=jax.ShapeDtypeStruct(routes.shape, f32),
        compiler_params=params(),
        name="place",
    )(routes, ranks, scores)


def local(tokens, grad_out, combine, routes, w_gate, w_up, w_down):
    experts, groups = lax.axis_size("expert"), lax.axis_size("dp")
    hidden = w_gate.shape[1]
    me = lax.axis_index("dp").astype(i32).reshape(1)
    by_slot = routes.T
    packed = pack(by_slot, combine.T, tokens, grad_out, experts)
    recv = lax.all_to_all(packed, "expert", split_axis=0, concat_axis=0, tiled=True)
    part, own, rows_x, rows_dy, probs = project(me, recv, stage(w_gate, w_up, w_down), groups)
    parts = lax.all_to_all(part, "dp", split_axis=0, concat_axis=0, tiled=True)
    mine = terms(me, parts, own, probs)
    rows = lax.all_gather(mine, "dp", axis=0, tiled=False)
    thirds = rows[:, : 3 * SUB, 3 * hidden :].astype(f32).reshape(groups, 3, SUB, LANES)
    scores = (thirds[:, 0] + thirds[:, 1] + thirds[:, 2]).reshape(experts, 1, LANES)
    returned = lax.all_to_all(scores, "expert", split_axis=0, concat_axis=0, tiled=True)
    *grads, ranks = outer(by_slot, rows, rows_x, rows_dy, hidden, experts)
    return tuple(grads) + (place(by_slot, ranks, returned.reshape(experts, LANES)).T,)


def solution(mesh):
    placed = (
        P("expert", "dp"),
        P("expert", "dp"),
        P("expert", None),
        P("expert", None),
        P("expert", None, "dp"),
        P("expert", None, "dp"),
        P("expert", None, "dp"),
    )
    return jax.shard_map(
        local,
        mesh=mesh,
        in_specs=placed,
        out_specs=(
            P("expert", None, "dp"),
            P("expert", None, "dp"),
            P("expert", None, "dp"),
            P("expert", None),
        ),
        check_vma=False,
    )
```

```python
import functools

import jax
import jax.numpy as jnp
from jax import lax
from jax.experimental import pallas as pl
from jax.experimental.pallas import tpu as pltpu
from jax.sharding import PartitionSpec as P

bf16, f32, i32 = jnp.bfloat16, jnp.float32, jnp.int32
LANES, SUB = 128, 8
TERM = 16
CAP = 9
LIMIT = 32 * 2**20
WHOLE = 64 * 2**20 - 2**19


def params(limit=LIMIT):
    return pltpu.CompilerParams(vmem_limit_bytes=limit)


def iota(shape, dim):
    return lax.broadcasted_iota(i32, shape, dim)


def mm(a, b, contract=((1,), (0,))):
    return lax.dot_general(a, b, (contract, ((), ())), preferred_element_type=f32)


def copies(pairs, sems):
    return [pltpu.make_async_copy(src, dst, sems.at[i]) for i, (src, dst) in enumerate(pairs)]


def rank_of(routes, experts, toks):
    e = iota((experts, toks), 0)
    first, second = e == routes[0:1, :], e == routes[1:2, :]
    named = first | second
    hot = jnp.where(named, 1.0, 0.0).astype(bf16)
    before = jnp.where(iota((toks, toks), 0) < iota((toks, toks), 1), 1.0, 0.0).astype(bf16)
    return first, second, jnp.where(named, mm(hot, before), -1.0)


def pack_kernel(routes_h, combine_h, tokens_h, grads_h, out_h, routes, combine, tokens, grads, out, last, ins, outs):
    experts = out.shape[0]
    toks, width = tokens.shape
    blocks = width // LANES
    half = blocks * SUB
    arriving = copies(
        [(routes_h, routes), (combine_h, combine), (tokens_h, tokens), (grads_h, grads)], ins
    )
    for c in arriving:
        c.start()
    arriving[0].wait()
    first, second, rank = rank_of(routes, experts, toks)
    slot = iota((experts, SUB, toks), 1)
    spread = jnp.broadcast_to(rank[:, None, :], (experts, SUB, toks))
    pick = jnp.where(spread == slot.astype(f32), 1.0, 0.0)
    pick = pick.reshape(experts * SUB, toks).astype(bf16)
    ninth = jnp.where(rank == float(SUB), 1.0, 0.0).astype(bf16)
    pieces = [slice(0, half), slice(half, 2 * half), slice(2 * half, 2 * half + 2 * SUB)]
    leaving = copies([(out.at[:, p], out_h.at[:, p]) for p in pieces], outs)
    last[...] = jnp.zeros(last.shape, f32)
    for i, source in enumerate((tokens, grads)):
        arriving[2 + i].wait()
        rows = mm(pick, source[...])
        for c in range(blocks):
            tile = rows[:, c * LANES : (c + 1) * LANES].reshape(experts, SUB, LANES)
            at = i * half + c * SUB
            out[:, at : at + SUB, :] = tile.astype(bf16)
        leaving[i].start()
        rows = mm(ninth, source[...])
        for c in range(blocks):
            place = i * blocks + c
            last[place // SUB, pl.ds(place % SUB, experts, stride=SUB), :] = rows[:, c * LANES : (c + 1) * LANES]
    arriving[1].wait()
    prob = combine[...].astype(f32)
    prob = jnp.where(first, prob[0:1, :], jnp.where(second, prob[1:2, :], 0.0))
    lane = iota((experts, LANES), 1)
    row = jnp.zeros((experts, LANES), f32)
    for r in range(CAP):
        value = jnp.sum(jnp.where(rank == float(r), prob, 0.0), axis=1, keepdims=True)
        row = jnp.where(lane == r, value, row)
    place = 2 * blocks
    last[place // SUB, pl.ds(place % SUB, experts, stride=SUB), :] = row
    for k in range(2):
        at = 2 * half + k * SUB
        out[:, at : at + SUB, :] = last[k].reshape(experts, SUB, LANES).astype(bf16)
    leaving[2].start()
    for c in leaving:
        c.wait()


def pack(routes, combine, tokens, grads, experts):
    toks, width = tokens.shape
    shape = (experts, (2 * width // LANES) * SUB + 2 * SUB, LANES)
    args = (routes, combine, tokens, grads)
    return pl.pallas_call(
        pack_kernel,
        in_specs=[pl.BlockSpec(memory_space=pltpu.HBM)] * 4,
        out_specs=pl.BlockSpec(memory_space=pltpu.HBM),
        out_shape=jax.ShapeDtypeStruct(shape, bf16),
        scratch_shapes=[pltpu.VMEM(a.shape, a.dtype) for a in args]
        + [
            pltpu.VMEM(shape, bf16),
            pltpu.VMEM((2, experts * SUB, LANES), f32),
            pltpu.SemaphoreType.DMA((4,)),
            pltpu.SemaphoreType.DMA((3,)),
        ],
        compiler_params=params(WHOLE),
        name="pack",
    )(*args)


def stage_kernel(gate, up, down, out):
    for i, weight in enumerate((gate, up, down)):
        out[i] = weight[0].astype(f32).T.astype(bf16)


def stage(*weights):
    _, hidden, width = weights[0].shape
    return pl.pallas_call(
        stage_kernel,
        out_shape=jax.ShapeDtypeStruct((len(weights), width, hidden), bf16),
        compiler_params=params(),
        cost_estimate=pl.CostEstimate(
            flops=3 * width * hidden, bytes_accessed=12 * width * hidden, transcendentals=0
        ),
        name="stage",
    )(*weights)


def project_kernel(me, recv, weights, part, own, rows_x, rows_dy, probs, last):
    experts = recv.shape[0]
    groups, count, _ = part.shape
    _, width, hidden = weights.shape
    blocks = width // LANES
    main = experts * SUB
    share = main // groups

    def tile(at):
        return recv[:, at : at + SUB, :].astype(f32).reshape(main, LANES)

    for k in range(2):
        last[k] = tile((2 * blocks + k) * SUB)

    def taken(place):
        return last[place // SUB, pl.ds(place % SUB, experts, stride=SUB), :]

    probs[...] = taken(2 * blocks)
    for i, rows in enumerate((rows_x, rows_dy)):
        for c in range(blocks):
            lanes = slice(c * LANES, (c + 1) * LANES)
            rows[0:main, lanes] = tile((i * blocks + c) * SUB).astype(bf16)
            rows[main:, lanes] = taken(i * blocks + c).astype(bf16)
    for i, rows in enumerate((rows_x, rows_x, rows_dy)):
        lanes = slice(i * hidden, (i + 1) * hidden)
        value = mm(rows[...], weights[i])
        for j in range(groups):
            piece = jnp.concatenate(
                [value[j * share : (j + 1) * share], value[main + j * SUB : main + (j + 1) * SUB]]
            )
            part[j, :, lanes] = piece.astype(bf16)

            @pl.when(me[0] == j)
            def _(piece=piece, lanes=lanes):
                own[:, lanes] = piece


def project(me, recv, weights, groups):
    experts = recv.shape[0]
    _, width, hidden = weights.shape
    total = experts * CAP
    count = total // groups
    vmem = pl.BlockSpec(memory_space=pltpu.VMEM)
    return pl.pallas_call(
        project_kernel,
        in_specs=[pl.BlockSpec(memory_space=pltpu.SMEM)] + [vmem] * 2,
        out_shape=(
            jax.ShapeDtypeStruct((groups, count, 3 * hidden), bf16),
            jax.ShapeDtypeStruct((count, 3 * hidden), f32),
            jax.ShapeDtypeStruct((total, width), bf16),
            jax.ShapeDtypeStruct((total, width), bf16),
            jax.ShapeDtypeStruct((experts, LANES), f32),
        ),
        scratch_shapes=[pltpu.VMEM((2, experts * SUB, LANES), f32)],
        compiler_params=params(),
        name="project",
    )(me, recv, weights)


def terms_kernel(me, parts, own, probs, out):
    groups, count, _ = parts.shape
    hidden = parts.shape[2] // 3
    main = count - SUB
    near = probs[pl.ds(pl.multiple_of(me[0] * SUB, SUB), SUB), :]
    lane = iota((SUB, SUB, LANES), 2)
    spread = jnp.broadcast_to(near[:, None, :], (SUB, SUB, LANES))
    picked = jnp.sum(jnp.where(lane == iota((SUB, SUB, LANES), 1), spread, 0.0), axis=2, keepdims=True)
    ninth = jnp.sum(jnp.where(iota((SUB, LANES), 1) == SUB, near, 0.0), axis=1, keepdims=True)
    weight = jnp.concatenate([picked.reshape(main, 1), ninth])

    def total(i):
        lanes = slice(i * hidden, (i + 1) * hidden)
        value = own[:, lanes]
        for j in range(groups):
            value = value + jnp.where(me[0] == j, 0.0, parts[j, :, lanes].astype(f32))
        return value

    gate_pre, up_pre, grad_hid = total(0), total(1), total(2)
    sig = jax.nn.sigmoid(gate_pre)
    silu_out = gate_pre * sig
    inner = silu_out * up_pre
    scaled = weight * grad_hid
    rows = (
        scaled * up_pre * (sig * (1.0 + gate_pre * (1.0 - sig))),
        scaled * silu_out,
        weight * inner,
    )
    per = hidden // LANES
    for i in range(3 * per):
        block = rows[i // per][:, i % per * LANES : (i % per + 1) * LANES].astype(bf16)
        for j in range(out.shape[0]):
            out[j, i * count : (i + 1) * count, :] = block
    score = jnp.sum(inner * grad_hid, axis=1, keepdims=True)
    cube = (SUB, SUB, LANES)
    lane = iota(cube, 2)
    direct = jnp.broadcast_to(score[:main].reshape(SUB, SUB, 1), cube)
    table = jnp.sum(jnp.where(lane % TERM == iota(cube, 1), direct, 0.0), axis=1)
    lane = iota((SUB, LANES), 1)
    table = jnp.where(lane % TERM == SUB, score[main:], table)
    high = table.astype(bf16).astype(f32)
    middle = (table - high).astype(bf16).astype(f32)
    low = table - high - middle
    table = jnp.where(lane < TERM, high, jnp.where(lane < 2 * TERM, middle, low))
    for j in range(out.shape[0]):
        out[j, 3 * per * count :, :] = table.astype(bf16)


def terms(me, parts, own, probs, times):
    count, wide = own.shape
    vmem = pl.BlockSpec(memory_space=pltpu.VMEM)
    return pl.pallas_call(
        terms_kernel,
        in_specs=[pl.BlockSpec(memory_space=pltpu.SMEM)] + [vmem] * 3,
        out_shape=jax.ShapeDtypeStruct((times, count * wide // LANES + SUB, LANES), bf16),
        compiler_params=params(),
        name="terms",
    )(me, parts, own, probs)


def outer_kernel(routes, rows, rows_x, rows_dy, gate, up, down, ranks):
    groups = rows.shape[0]
    hidden = gate.shape[1]
    per = hidden // LANES
    count = (rows.shape[1] - SUB) // (3 * per)
    main = count - SUB

    def block(i):
        at = i * count
        direct = rows[:, at : at + main, :].astype(f32).reshape(groups * main, LANES)
        ninth = rows[:, at + main : at + count, :].astype(f32).reshape(groups * SUB, LANES)
        return jnp.concatenate([direct, ninth]).astype(bf16)

    for i, (other, out) in enumerate(((rows_x, gate), (rows_x, up), (rows_dy, down))):
        value = jnp.concatenate([block(i * per + c) for c in range(per)], axis=1)
        out[0] = mm(value, other[...], ((0,), (0,))).astype(bf16)
    ranks[...] = rank_of(routes, *ranks.shape)[2]


def outer(routes, rows, rows_x, rows_dy, hidden, experts):
    total, width = rows_x.shape
    return pl.pallas_call(
        outer_kernel,
        out_shape=(jax.ShapeDtypeStruct((1, hidden, width), bf16),) * 3
        + (jax.ShapeDtypeStruct((experts, routes.shape[1]), f32),),
        compiler_params=params(),
        cost_estimate=pl.CostEstimate(
            flops=6 * total * width * hidden, bytes_accessed=8 * total * width, transcendentals=0
        ),
        name="outer",
    )(routes, rows, rows_x, rows_dy)


def place_kernel(routes, ranks, scores, out):
    experts, toks = ranks.shape
    rank = ranks[...]
    table = scores[:, 0:TERM] + scores[:, TERM : 2 * TERM] + scores[:, 2 * TERM : 3 * TERM]
    value = jnp.zeros((experts, toks), f32)
    for r in range(CAP):
        value = jnp.where(rank == float(r), table[:, r : r + 1], value)
    e = iota((experts, toks), 0)
    for k in range(2):
        out[k : k + 1, :] = jnp.sum(
            jnp.where(e == routes[k : k + 1, :], value, 0.0), axis=0, keepdims=True
        )


def place(routes, ranks, scores):
    return pl.pallas_call(
        place_kernel,
        out_shape=jax.ShapeDtypeStruct(routes.shape, f32),
        compiler_params=params(),
        name="place",
    )(routes, ranks, scores)


def local(tokens, grad_out, combine, routes, w_gate, w_up, w_down):
    experts, groups = lax.axis_size("expert"), lax.axis_size("dp")
    hidden = w_gate.shape[1]
    y, core = lax.axis_index("dp").astype(i32), lax.axis_index("expert").astype(i32) & 1
    me = jnp.where(core == 1, groups - 1 - y, y).reshape(1)
    by_slot = routes.T
    packed = pack(by_slot, combine.T, tokens, grad_out, experts)
    recv = lax.all_to_all(packed, "expert", split_axis=0, concat_axis=0, tiled=True)
    part, own, rows_x, rows_dy, probs = project(me, recv, stage(w_gate, w_up, w_down), groups)
    both = ("expert", "dp")
    lines = [
        [e * groups + (groups - 1 - j if e % 2 else j) for j in range(groups)] for e in range(experts)
    ]

    def exchange(pieces):
        return lax.all_to_all(
            pieces, both, split_axis=0, concat_axis=0, tiled=True, axis_index_groups=lines
        )

    def by_source(rows):
        return rows, rows[:, -SUB:, :].astype(f32).reshape(experts, 1, LANES)

    def even(part, own, probs):
        return by_source(exchange(terms(me, exchange(part), own, probs, groups)))

    def odd(part, own, probs):
        mine = terms(me, exchange(part), own, probs, 1)
        return by_source(lax.all_gather(mine, both, axis=0, tiled=True, axis_index_groups=lines))

    rows, scores = lax.cond(core == 0, even, odd, part, own, probs)
    returned = lax.all_to_all(scores, "expert", split_axis=0, concat_axis=0, tiled=True)
    *grads, ranks = outer(by_slot, rows, rows_x, rows_dy, hidden, experts)
    return tuple(grads) + (place(by_slot, ranks, returned.reshape(experts, LANES)).T,)


def solution(mesh):
    placed = (
        P("expert", "dp"),
        P("expert", "dp"),
        P("expert", None),
        P("expert", None),
        P("expert", None, "dp"),
        P("expert", None, "dp"),
        P("expert", None, "dp"),
    )
    return jax.shard_map(
        local,
        mesh=mesh,
        in_specs=placed,
        out_specs=(
            P("expert", None, "dp"),
            P("expert", None, "dp"),
            P("expert", None, "dp"),
            P("expert", None),
        ),
        check_vma=False,
    )
```

```python
import functools

import jax
import jax.numpy as jnp
from jax import lax
from jax.experimental import pallas as pl
from jax.experimental.pallas import tpu as pltpu
from jax.sharding import PartitionSpec as P

bf16, f32, i32 = jnp.bfloat16, jnp.float32, jnp.int32
LANES, SUB = 128, 8
TERM = 16
TURN = 5
CAP = 9
LIMIT = 32 * 2**20
WHOLE = 64 * 2**20 - 2**19


def params(limit=LIMIT):
    return pltpu.CompilerParams(vmem_limit_bytes=limit)


def iota(shape, dim):
    return lax.broadcasted_iota(i32, shape, dim)


def mm(a, b, contract=((1,), (0,))):
    return lax.dot_general(a, b, (contract, ((), ())), preferred_element_type=f32)


def copies(pairs, sems):
    return [pltpu.make_async_copy(src, dst, sems.at[i]) for i, (src, dst) in enumerate(pairs)]


def rank_of(routes, experts, toks):
    e = iota((experts, toks), 0)
    first, second = e == routes[0:1, :], e == routes[1:2, :]
    named = first | second
    hot = jnp.where(named, 1.0, 0.0).astype(bf16)
    before = jnp.where(iota((toks, toks), 0) < iota((toks, toks), 1), 1.0, 0.0).astype(bf16)
    return first, second, jnp.where(named, mm(hot, before), -1.0)


def pack_kernel(routes_h, combine_h, tokens_h, grads_h, out_h, routes, combine, tokens, grads, out, last, ins, outs):
    experts = out.shape[0]
    toks, width = tokens.shape
    blocks = width // LANES
    half = blocks * SUB
    arriving = copies(
        [(routes_h, routes), (combine_h, combine), (tokens_h, tokens), (grads_h, grads)], ins
    )
    for c in arriving:
        c.start()
    arriving[0].wait()
    first, second, rank = rank_of(routes, experts, toks)
    slot = iota((experts, SUB, toks), 1)
    spread = jnp.broadcast_to(rank[:, None, :], (experts, SUB, toks))
    pick = jnp.where(spread == slot.astype(f32), 1.0, 0.0)
    pick = pick.reshape(experts * SUB, toks).astype(bf16)
    ninth = jnp.where(rank == float(SUB), 1.0, 0.0).astype(bf16)
    pieces = [slice(0, half), slice(half, 2 * half), slice(2 * half, 2 * half + 2 * SUB)]
    leaving = copies([(out.at[:, p], out_h.at[:, p]) for p in pieces], outs)
    last[...] = jnp.zeros(last.shape, f32)
    for i, source in enumerate((tokens, grads)):
        arriving[2 + i].wait()
        rows = mm(pick, source[...])
        for c in range(blocks):
            tile = rows[:, c * LANES : (c + 1) * LANES].reshape(experts, SUB, LANES)
            at = i * half + c * SUB
            out[:, at : at + SUB, :] = tile.astype(bf16)
        leaving[i].start()
        rows = mm(ninth, source[...])
        for c in range(blocks):
            place = i * blocks + c
            last[place // SUB, pl.ds(place % SUB, experts, stride=SUB), :] = rows[:, c * LANES : (c + 1) * LANES]
    arriving[1].wait()
    prob = combine[...].astype(f32)
    prob = jnp.where(first, prob[0:1, :], jnp.where(second, prob[1:2, :], 0.0))
    lane = iota((experts, LANES), 1)
    row = jnp.zeros((experts, LANES), f32)
    for r in range(CAP):
        value = jnp.sum(jnp.where(rank == float(r), prob, 0.0), axis=1, keepdims=True)
        row = jnp.where(lane == r, value, row)
    place = 2 * blocks
    last[place // SUB, pl.ds(place % SUB, experts, stride=SUB), :] = row
    for k in range(2):
        at = 2 * half + k * SUB
        out[:, at : at + SUB, :] = last[k].reshape(experts, SUB, LANES).astype(bf16)
    leaving[2].start()
    for c in leaving:
        c.wait()


def pack(routes, combine, tokens, grads, experts):
    toks, width = tokens.shape
    shape = (experts, (2 * width // LANES) * SUB + 2 * SUB, LANES)
    args = (routes, combine, tokens, grads)
    return pl.pallas_call(
        pack_kernel,
        in_specs=[pl.BlockSpec(memory_space=pltpu.HBM)] * 4,
        out_specs=pl.BlockSpec(memory_space=pltpu.HBM),
        out_shape=jax.ShapeDtypeStruct(shape, bf16),
        scratch_shapes=[pltpu.VMEM(a.shape, a.dtype) for a in args]
        + [
            pltpu.VMEM(shape, bf16),
            pltpu.VMEM((2, experts * SUB, LANES), f32),
            pltpu.SemaphoreType.DMA((4,)),
            pltpu.SemaphoreType.DMA((3,)),
        ],
        compiler_params=params(WHOLE),
        name="pack",
    )(*args)


def stage_kernel(gate, up, down, out):
    for i, weight in enumerate((gate, up, down)):
        out[i] = weight[0].astype(f32).T.astype(bf16)


def stage(*weights):
    _, hidden, width = weights[0].shape
    return pl.pallas_call(
        stage_kernel,
        out_shape=jax.ShapeDtypeStruct((len(weights), width, hidden), bf16),
        compiler_params=params(),
        cost_estimate=pl.CostEstimate(
            flops=3 * width * hidden, bytes_accessed=12 * width * hidden, transcendentals=0
        ),
        name="stage",
    )(*weights)


def unpack(recv, rows_x, rows_dy, last):
    experts = recv.shape[0]
    blocks = rows_x.shape[1] // LANES
    main = experts * SUB

    def tile(at):
        return recv[:, at : at + SUB, :].astype(f32).reshape(main, LANES)

    for k in range(2):
        last[k] = tile((2 * blocks + k) * SUB)

    def taken(place):
        return last[place // SUB, pl.ds(place % SUB, experts, stride=SUB), :]

    for i, rows in enumerate((rows_x, rows_dy)):
        for c in range(blocks):
            lanes = slice(c * LANES, (c + 1) * LANES)
            rows[0:main, lanes] = tile((i * blocks + c) * SUB).astype(bf16)
            rows[main:, lanes] = taken(i * blocks + c).astype(bf16)
    return taken(2 * blocks)


def project_kernel(me, recv, weights, part, own, probs, rows_x, rows_dy, last):
    groups = part.shape[0]
    _, width, hidden = weights.shape
    main = recv.shape[0] * SUB
    share = main // groups
    probs[...] = unpack(recv, rows_x, rows_dy, last)
    for i, rows in enumerate((rows_x, rows_x, rows_dy)):
        lanes = slice(i * hidden, (i + 1) * hidden)
        value = mm(rows[...], weights[i])
        for j in range(groups):
            piece = jnp.concatenate(
                [value[j * share : (j + 1) * share], value[main + j * SUB : main + (j + 1) * SUB]]
            )
            part[j, :, lanes] = piece.astype(bf16)

            @pl.when(me[0] == j)
            def _(piece=piece, lanes=lanes):
                own[:, lanes] = piece


def unpacked(experts, width):
    rows = pltpu.VMEM((experts * CAP, width), bf16)
    return [rows, rows, pltpu.VMEM((2, experts * SUB, LANES), f32)]


def project(me, recv, weights, groups):
    experts = recv.shape[0]
    _, width, hidden = weights.shape
    total = experts * CAP
    count = total // groups
    vmem = pl.BlockSpec(memory_space=pltpu.VMEM)
    return pl.pallas_call(
        project_kernel,
        in_specs=[pl.BlockSpec(memory_space=pltpu.SMEM)] + [vmem] * 2,
        out_shape=(
            jax.ShapeDtypeStruct((groups, count, 3 * hidden), bf16),
            jax.ShapeDtypeStruct((count, 3 * hidden), f32),
            jax.ShapeDtypeStruct((experts, LANES), f32),
        ),
        scratch_shapes=unpacked(experts, width),
        compiler_params=params(),
        name="project",
    )(me, recv, weights)


def terms_kernel(me, parts, own, probs, out):
    groups, count, _ = parts.shape
    hidden = parts.shape[2] // 3
    main = count - SUB
    near = probs[pl.ds(pl.multiple_of(me[0] * SUB, SUB), SUB), :]
    lane = iota((SUB, SUB, LANES), 2)
    spread = jnp.broadcast_to(near[:, None, :], (SUB, SUB, LANES))
    picked = jnp.sum(jnp.where(lane == iota((SUB, SUB, LANES), 1), spread, 0.0), axis=2, keepdims=True)
    ninth = jnp.sum(jnp.where(iota((SUB, LANES), 1) == SUB, near, 0.0), axis=1, keepdims=True)
    weight = jnp.concatenate([picked.reshape(main, 1), ninth])

    def total(i):
        lanes = slice(i * hidden, (i + 1) * hidden)
        value = own[:, lanes]
        for j in range(groups):
            value = value + jnp.where(me[0] == j, 0.0, parts[j, :, lanes].astype(f32))
        return value

    gate_pre, up_pre, grad_hid = total(0), total(1), total(2)
    sig = jax.nn.sigmoid(gate_pre)
    silu_out = gate_pre * sig
    inner = silu_out * up_pre
    scaled = weight * grad_hid
    rows = (
        scaled * up_pre * (sig * (1.0 + gate_pre * (1.0 - sig))),
        scaled * silu_out,
        weight * inner,
    )
    per = hidden // LANES
    for i in range(3 * per):
        block = rows[i // per][:, i % per * LANES : (i % per + 1) * LANES].astype(bf16)
        for j in range(out.shape[0]):
            out[j, i * count : (i + 1) * count, :] = block
    score = jnp.sum(inner * grad_hid, axis=1, keepdims=True)
    cube = (SUB, SUB, LANES)
    lane = iota(cube, 2)
    direct = jnp.broadcast_to(score[:main].reshape(SUB, SUB, 1), cube)
    table = jnp.sum(jnp.where(lane % TERM == iota(cube, 1), direct, 0.0), axis=1)
    lane = iota((SUB, LANES), 1)
    table = jnp.where(lane % TERM == SUB, score[main:], table)
    high = table.astype(bf16).astype(f32)
    middle = (table - high).astype(bf16).astype(f32)
    low = table - high - middle
    table = jnp.where(lane < TERM, high, jnp.where(lane < 2 * TERM, middle, low))
    for j in range(out.shape[0]):
        out[j, 3 * per * count :, :] = table.astype(bf16)


def terms(me, parts, own, probs, times):
    count, wide = own.shape
    vmem = pl.BlockSpec(memory_space=pltpu.VMEM)
    return pl.pallas_call(
        terms_kernel,
        in_specs=[pl.BlockSpec(memory_space=pltpu.SMEM)] + [vmem] * 3,
        out_shape=jax.ShapeDtypeStruct((times, count * wide // LANES + SUB, LANES), bf16),
        compiler_params=params(),
        name="terms",
    )(me, parts, own, probs)


def outer_kernel(routes, rows, recv, gate, up, down, ranks, rows_x, rows_dy, last):
    groups = rows.shape[0]
    hidden = gate.shape[1]
    per = hidden // LANES
    count = (rows.shape[1] - SUB) // (3 * per)
    main = count - SUB
    unpack(recv, rows_x, rows_dy, last)

    def block(i):
        at = i * count
        direct = rows[:, at : at + main, :].astype(f32).reshape(groups * main, LANES)
        ninth = rows[:, at + main : at + count, :].astype(f32).reshape(groups * SUB, LANES)
        return jnp.concatenate([direct, ninth]).astype(bf16)

    for i, (other, out) in enumerate(((rows_x, gate), (rows_x, up), (rows_dy, down))):
        value = jnp.concatenate([block(i * per + c) for c in range(per)], axis=1)
        out[0] = mm(value, other[...], ((0,), (0,))).astype(bf16)
    ranks[...] = rank_of(routes, *ranks.shape)[2]


def outer(routes, rows, recv, hidden, width):
    experts = recv.shape[0]
    total = experts * CAP
    return pl.pallas_call(
        outer_kernel,
        out_shape=(jax.ShapeDtypeStruct((1, hidden, width), bf16),) * 3
        + (jax.ShapeDtypeStruct((experts, routes.shape[1]), f32),),
        scratch_shapes=unpacked(experts, width),
        compiler_params=params(),
        cost_estimate=pl.CostEstimate(
            flops=6 * total * width * hidden, bytes_accessed=8 * total * width, transcendentals=0
        ),
        name="outer",
    )(routes, rows, recv)


def place_kernel(routes, ranks, scores, out):
    experts, toks = ranks.shape
    rank = ranks[...]
    table = scores[:, 0:TERM] + scores[:, TERM : 2 * TERM] + scores[:, 2 * TERM : 3 * TERM]
    value = jnp.zeros((experts, toks), f32)
    for r in range(CAP):
        value = jnp.where(rank == float(r), table[:, r : r + 1], value)
    e = iota((experts, toks), 0)
    for k in range(2):
        out[k : k + 1, :] = jnp.sum(
            jnp.where(e == routes[k : k + 1, :], value, 0.0), axis=0, keepdims=True
        )


def place(routes, ranks, scores):
    return pl.pallas_call(
        place_kernel,
        out_shape=jax.ShapeDtypeStruct(routes.shape, f32),
        compiler_params=params(),
        name="place",
    )(routes, ranks, scores)


def local(tokens, grad_out, combine, routes, w_gate, w_up, w_down):
    experts, groups = lax.axis_size("expert"), lax.axis_size("dp")
    hidden = w_gate.shape[1]
    y, core = lax.axis_index("dp").astype(i32), lax.axis_index("expert").astype(i32) & 1
    me = jnp.where(core == 1, lax.rem(TURN + groups - y, groups), y).reshape(1)
    by_slot = routes.T
    packed = pack(by_slot, combine.T, tokens, grad_out, experts)
    recv = lax.all_to_all(packed, "expert", split_axis=0, concat_axis=0, tiled=True)
    part, own, probs = project(me, recv, stage(w_gate, w_up, w_down), groups)
    both = ("expert", "dp")
    lines = [
        [e * groups + ((TURN - j) % groups if e % 2 else j) for j in range(groups)] for e in range(experts)
    ]

    def exchange(pieces):
        return lax.all_to_all(
            pieces, both, split_axis=0, concat_axis=0, tiled=True, axis_index_groups=lines
        )

    def by_source(rows):
        return rows, rows[:, -SUB:, :].astype(f32).reshape(experts, 1, LANES)

    def even(part, own, probs):
        return by_source(exchange(terms(me, exchange(part), own, probs, groups)))

    def odd(part, own, probs):
        mine = terms(me, exchange(part), own, probs, 1)
        return by_source(lax.all_gather(mine, both, axis=0, tiled=True, axis_index_groups=lines))

    rows, scores = lax.cond(core == 0, even, odd, part, own, probs)
    returned = lax.all_to_all(scores, "expert", split_axis=0, concat_axis=0, tiled=True)
    *grads, ranks = outer(by_slot, rows, recv, hidden, tokens.shape[1])
    return tuple(grads) + (place(by_slot, ranks, returned.reshape(experts, LANES)).T,)


def solution(mesh):
    placed = (
        P("expert", "dp"),
        P("expert", "dp"),
        P("expert", None),
        P("expert", None),
        P("expert", None, "dp"),
        P("expert", None, "dp"),
        P("expert", None, "dp"),
    )
    return jax.shard_map(
        local,
        mesh=mesh,
        in_specs=placed,
        out_specs=(
            P("expert", None, "dp"),
            P("expert", None, "dp"),
            P("expert", None, "dp"),
            P("expert", None),
        ),
        check_vma=False,
    )
```

```python
import functools

import jax
import jax.numpy as jnp
from jax import lax
from jax.experimental import pallas as pl
from jax.experimental.pallas import tpu as pltpu
from jax.sharding import PartitionSpec as P

bf16, f32, i32 = jnp.bfloat16, jnp.float32, jnp.int32
LANES, SUB = 128, 8
TERM = 16
TURN = 5
CAP = 9
LIMIT = 32 * 2**20
WHOLE = 64 * 2**20 - 2**19


def params(limit=LIMIT):
    return pltpu.CompilerParams(vmem_limit_bytes=limit)


def iota(shape, dim):
    return lax.broadcasted_iota(i32, shape, dim)


def mm(a, b, contract=((1,), (0,))):
    return lax.dot_general(a, b, (contract, ((), ())), preferred_element_type=f32)


def copies(pairs, sems):
    return [pltpu.make_async_copy(src, dst, sems.at[i]) for i, (src, dst) in enumerate(pairs)]


def rank_of(routes, experts, toks):
    e = iota((experts, toks), 0)
    first, second = e == routes[0:1, :], e == routes[1:2, :]
    named = first | second
    hot = jnp.where(named, 1.0, 0.0).astype(bf16)
    before = jnp.where(iota((toks, toks), 0) < iota((toks, toks), 1), 1.0, 0.0).astype(bf16)
    return first, second, jnp.where(named, mm(hot, before), -1.0)


def pack_kernel(routes_h, combine_h, tokens_h, grads_h, out_h, routes, combine, tokens, grads, out, last, ins, outs):
    experts = out.shape[0]
    toks, width = tokens.shape
    blocks = width // LANES
    half = blocks * SUB
    arriving = copies(
        [(routes_h, routes), (combine_h, combine), (tokens_h, tokens), (grads_h, grads)], ins
    )
    for c in arriving:
        c.start()
    arriving[0].wait()
    first, second, rank = rank_of(routes, experts, toks)
    slot = iota((experts, SUB, toks), 1)
    spread = jnp.broadcast_to(rank[:, None, :], (experts, SUB, toks))
    pick = jnp.where(spread == slot.astype(f32), 1.0, 0.0)
    pick = pick.reshape(experts * SUB, toks).astype(bf16)
    ninth = jnp.where(rank == float(SUB), 1.0, 0.0).astype(bf16)
    pieces = [slice(at, at + 2 * SUB) for at in range(0, 2 * half + 2 * SUB, 2 * SUB)]
    leaving = copies([(out.at[:, p], out_h.at[:, p]) for p in pieces], outs)
    last[...] = jnp.zeros(last.shape, f32)
    arriving[1].wait()
    prob = combine[...].astype(f32)
    prob = jnp.where(first, prob[0:1, :], jnp.where(second, prob[1:2, :], 0.0))
    lane = iota((experts, LANES), 1)
    row = jnp.zeros((experts, LANES), f32)
    for r in range(CAP):
        value = jnp.sum(jnp.where(rank == float(r), prob, 0.0), axis=1, keepdims=True)
        row = jnp.where(lane == r, value, row)
    place = 2 * blocks
    last[place // SUB, pl.ds(place % SUB, experts, stride=SUB), :] = row
    for i, source in enumerate((tokens, grads)):
        arriving[2 + i].wait()
        rows = mm(pick, source[...])
        for c in range(blocks):
            tile = rows[:, c * LANES : (c + 1) * LANES].reshape(experts, SUB, LANES)
            at = i * half + c * SUB
            out[:, at : at + SUB, :] = tile.astype(bf16)
            if c % 2:
                leaving[(i * blocks + c) // 2].start()
        rows = mm(ninth, source[...])
        for c in range(blocks):
            place = i * blocks + c
            last[place // SUB, pl.ds(place % SUB, experts, stride=SUB), :] = rows[:, c * LANES : (c + 1) * LANES]
    for k in range(2):
        at = 2 * half + k * SUB
        out[:, at : at + SUB, :] = last[k].reshape(experts, SUB, LANES).astype(bf16)
    leaving[-1].start()
    for c in leaving:
        c.wait()


def pack(routes, combine, tokens, grads, experts):
    toks, width = tokens.shape
    shape = (experts, (2 * width // LANES) * SUB + 2 * SUB, LANES)
    args = (routes, combine, tokens, grads)
    return pl.pallas_call(
        pack_kernel,
        in_specs=[pl.BlockSpec(memory_space=pltpu.HBM)] * 4,
        out_specs=pl.BlockSpec(memory_space=pltpu.HBM),
        out_shape=jax.ShapeDtypeStruct(shape, bf16),
        scratch_shapes=[pltpu.VMEM(a.shape, a.dtype) for a in args]
        + [
            pltpu.VMEM(shape, bf16),
            pltpu.VMEM((2, experts * SUB, LANES), f32),
            pltpu.SemaphoreType.DMA((4,)),
            pltpu.SemaphoreType.DMA((width // LANES + 1,)),
        ],
        compiler_params=params(WHOLE),
        name="pack",
    )(*args)


def stage_kernel(gate, up, down, out):
    for i, weight in enumerate((gate, up, down)):
        out[i] = weight[0].astype(f32).T.astype(bf16)


def stage(*weights):
    _, hidden, width = weights[0].shape
    return pl.pallas_call(
        stage_kernel,
        out_shape=jax.ShapeDtypeStruct((len(weights), width, hidden), bf16),
        compiler_params=params(),
        cost_estimate=pl.CostEstimate(
            flops=3 * width * hidden, bytes_accessed=12 * width * hidden, transcendentals=0
        ),
        name="stage",
    )(*weights)


def unpack(recv, rows_x, rows_dy, last):
    experts = recv.shape[0]
    blocks = rows_x.shape[1] // LANES
    main = experts * SUB

    def tile(at):
        return recv[:, at : at + SUB, :].reshape(main, LANES)

    for k in range(2):
        last[k] = tile((2 * blocks + k) * SUB).astype(f32)

    def taken(place):
        return last[place // SUB, pl.ds(place % SUB, experts, stride=SUB), :]

    for i, rows in enumerate((rows_x, rows_dy)):
        for c in range(blocks):
            lanes = slice(c * LANES, (c + 1) * LANES)
            rows[0:main, lanes] = tile((i * blocks + c) * SUB)
            rows[main:, lanes] = taken(i * blocks + c).astype(bf16)
    return taken(2 * blocks)


def project_kernel(me, recv, weights, part, own, probs, rows_x, rows_dy, last):
    groups = part.shape[0]
    _, width, hidden = weights.shape
    main = recv.shape[0] * SUB
    share = main // groups
    probs[...] = unpack(recv, rows_x, rows_dy, last)
    for i, rows in enumerate((rows_x, rows_x, rows_dy)):
        lanes = slice(i * hidden, (i + 1) * hidden)
        value = mm(rows[...], weights[i])
        for j in range(groups):
            piece = jnp.concatenate(
                [value[j * share : (j + 1) * share], value[main + j * SUB : main + (j + 1) * SUB]]
            )
            part[j, :, lanes] = piece.astype(bf16)

            @pl.when(me[0] == j)
            def _(piece=piece, lanes=lanes):
                own[:, lanes] = piece


def unpacked(experts, width):
    rows = pltpu.VMEM((experts * CAP, width), bf16)
    return [rows, rows, pltpu.VMEM((2, experts * SUB, LANES), f32)]


def project(me, recv, weights, groups):
    experts = recv.shape[0]
    _, width, hidden = weights.shape
    total = experts * CAP
    count = total // groups
    vmem = pl.BlockSpec(memory_space=pltpu.VMEM)
    return pl.pallas_call(
        project_kernel,
        in_specs=[pl.BlockSpec(memory_space=pltpu.SMEM)] + [vmem] * 2,
        out_shape=(
            jax.ShapeDtypeStruct((groups, count, 3 * hidden), bf16),
            jax.ShapeDtypeStruct((count, 3 * hidden), f32),
            jax.ShapeDtypeStruct((experts, LANES), f32),
        ),
        scratch_shapes=unpacked(experts, width),
        compiler_params=params(),
        name="project",
    )(me, recv, weights)


def terms_kernel(me, parts, own, probs, out):
    groups, count, _ = parts.shape
    hidden = parts.shape[2] // 3
    main = count - SUB
    near = probs[pl.ds(pl.multiple_of(me[0] * SUB, SUB), SUB), :]
    lane = iota((SUB, SUB, LANES), 2)
    spread = jnp.broadcast_to(near[:, None, :], (SUB, SUB, LANES))
    picked = jnp.sum(jnp.where(lane == iota((SUB, SUB, LANES), 1), spread, 0.0), axis=2, keepdims=True)
    ninth = jnp.sum(jnp.where(iota((SUB, LANES), 1) == SUB, near, 0.0), axis=1, keepdims=True)
    weight = jnp.concatenate([picked.reshape(main, 1), ninth])

    def total(i):
        lanes = slice(i * hidden, (i + 1) * hidden)
        value = own[:, lanes]
        for j in range(groups):
            value = value + jnp.where(me[0] == j, 0.0, parts[j, :, lanes].astype(f32))
        return value

    gate_pre, up_pre, grad_hid = total(0), total(1), total(2)
    sig = jax.nn.sigmoid(gate_pre)
    silu_out = gate_pre * sig
    inner = silu_out * up_pre
    scaled = weight * grad_hid
    rows = (
        scaled * up_pre * (sig * (1.0 + gate_pre * (1.0 - sig))),
        scaled * silu_out,
        weight * inner,
    )
    per = hidden // LANES
    for i in range(3 * per):
        block = rows[i // per][:, i % per * LANES : (i % per + 1) * LANES].astype(bf16)
        for j in range(out.shape[0]):
            out[j, i * count : (i + 1) * count, :] = block
    score = jnp.sum(inner * grad_hid, axis=1, keepdims=True)
    cube = (SUB, SUB, LANES)
    lane = iota(cube, 2)
    direct = jnp.broadcast_to(score[:main].reshape(SUB, SUB, 1), cube)
    table = jnp.sum(jnp.where(lane % TERM == iota(cube, 1), direct, 0.0), axis=1)
    lane = iota((SUB, LANES), 1)
    table = jnp.where(lane % TERM == SUB, score[main:], table)
    high = table.astype(bf16).astype(f32)
    middle = (table - high).astype(bf16).astype(f32)
    low = table - high - middle
    table = jnp.where(lane < TERM, high, jnp.where(lane < 2 * TERM, middle, low))
    for j in range(out.shape[0]):
        out[j, 3 * per * count :, :] = table.astype(bf16)


def terms(me, parts, own, probs, times):
    count, wide = own.shape
    vmem = pl.BlockSpec(memory_space=pltpu.VMEM)
    return pl.pallas_call(
        terms_kernel,
        in_specs=[pl.BlockSpec(memory_space=pltpu.SMEM)] + [vmem] * 3,
        out_shape=jax.ShapeDtypeStruct((times, count * wide // LANES + SUB, LANES), bf16),
        compiler_params=params(),
        name="terms",
    )(me, parts, own, probs)


def outer_kernel(routes, rows, recv, gate, up, down, ranks, rows_x, rows_dy, last):
    groups = rows.shape[0]
    hidden = gate.shape[1]
    per = hidden // LANES
    count = (rows.shape[1] - SUB) // (3 * per)
    main = count - SUB
    unpack(recv, rows_x, rows_dy, last)

    def block(i):
        at = i * count
        direct = rows[:, at : at + main, :].astype(f32).reshape(groups * main, LANES)
        ninth = rows[:, at + main : at + count, :].astype(f32).reshape(groups * SUB, LANES)
        return jnp.concatenate([direct, ninth]).astype(bf16)

    for i, (other, out) in enumerate(((rows_x, gate), (rows_x, up), (rows_dy, down))):
        value = jnp.concatenate([block(i * per + c) for c in range(per)], axis=1)
        out[0] = mm(value, other[...], ((0,), (0,))).astype(bf16)
    first, second, rank = rank_of(routes, recv.shape[0], routes.shape[1])
    for k, mine in enumerate((first, second)):
        ranks[k : k + 1, :] = jnp.sum(jnp.where(mine, rank, 0.0), axis=0, keepdims=True)


def outer(routes, rows, recv, hidden, width):
    experts = recv.shape[0]
    total = experts * CAP
    return pl.pallas_call(
        outer_kernel,
        out_shape=(jax.ShapeDtypeStruct((1, hidden, width), bf16),) * 3
        + (jax.ShapeDtypeStruct(routes.shape, f32),),
        scratch_shapes=unpacked(experts, width),
        compiler_params=params(),
        cost_estimate=pl.CostEstimate(
            flops=6 * total * width * hidden, bytes_accessed=8 * total * width, transcendentals=0
        ),
        name="outer",
    )(routes, rows, recv)


def place_kernel(routes, ranks, scores, out):
    experts, toks = scores.shape[0], routes.shape[1]
    table = scores[:, 0 : 3 * TERM].astype(bf16)
    e = iota((experts, toks), 0)
    slot = (iota((3 * TERM, toks), 0) & (TERM - 1)).astype(f32)
    for k in range(2):
        hot = jnp.where(e == routes[k : k + 1, :], 1.0, 0.0).astype(bf16)
        taken = mm(table, hot, ((0,), (0,)))
        taken = jnp.where(slot == ranks[k : k + 1, :], taken, 0.0)
        out[k : k + 1, :] = jnp.sum(taken, axis=0, keepdims=True)


def place(routes, ranks, scores):
    return pl.pallas_call(
        place_kernel,
        out_shape=jax.ShapeDtypeStruct(routes.shape, f32),
        compiler_params=params(),
        name="place",
    )(routes, ranks, scores)


def local(tokens, grad_out, combine, routes, w_gate, w_up, w_down):
    experts, groups = lax.axis_size("expert"), lax.axis_size("dp")
    hidden = w_gate.shape[1]
    y, core = lax.axis_index("dp").astype(i32), lax.axis_index("expert").astype(i32) & 1
    me = jnp.where(core == 1, lax.rem(TURN + groups - y, groups), y).reshape(1)
    by_slot = routes.T
    packed = pack(by_slot, combine.T, tokens, grad_out, experts)
    recv = lax.all_to_all(packed, "expert", split_axis=0, concat_axis=0, tiled=True)
    part, own, probs = project(me, recv, stage(w_gate, w_up, w_down), groups)
    both = ("expert", "dp")
    lines = [
        [e * groups + ((TURN - j) % groups if e % 2 else j) for j in range(groups)] for e in range(experts)
    ]

    def exchange(pieces):
        return lax.all_to_all(
            pieces, both, split_axis=0, concat_axis=0, tiled=True, axis_index_groups=lines
        )

    def by_source(rows):
        return rows, rows[:, -SUB:, :].astype(f32).reshape(experts, 1, LANES)

    def even(part, own, probs):
        return by_source(exchange(terms(me, exchange(part), own, probs, groups)))

    def odd(part, own, probs):
        mine = terms(me, exchange(part), own, probs, 1)
        return by_source(lax.all_gather(mine, both, axis=0, tiled=True, axis_index_groups=lines))

    rows, scores = lax.cond(core == 0, even, odd, part, own, probs)
    returned = lax.all_to_all(scores, "expert", split_axis=0, concat_axis=0, tiled=True)
    *grads, ranks = outer(by_slot, rows, recv, hidden, tokens.shape[1])
    return tuple(grads) + (place(by_slot, ranks, returned.reshape(experts, LANES)).T,)


def solution(mesh):
    placed = (
        P("expert", "dp"),
        P("expert", "dp"),
        P("expert", None),
        P("expert", None),
        P("expert", None, "dp"),
        P("expert", None, "dp"),
        P("expert", None, "dp"),
    )
    return jax.shard_map(
        local,
        mesh=mesh,
        in_specs=placed,
        out_specs=(
            P("expert", None, "dp"),
            P("expert", None, "dp"),
            P("expert", None, "dp"),
            P("expert", None),
        ),
        check_vma=False,
    )
```

```python
import functools

import jax
import jax.numpy as jnp
from jax import lax
from jax.experimental import pallas as pl
from jax.experimental.pallas import tpu as pltpu
from jax.sharding import PartitionSpec as P

bf16, f32, i32 = jnp.bfloat16, jnp.float32, jnp.int32
LANES, SUB = 128, 8
TERM = 16
TURN = 5
CAP = 9
LIMIT = 32 * 2**20
WHOLE = 64 * 2**20 - 2**19


def params(limit=LIMIT):
    return pltpu.CompilerParams(vmem_limit_bytes=limit)


def iota(shape, dim):
    return lax.broadcasted_iota(i32, shape, dim)


def mm(a, b, contract=((1,), (0,))):
    return lax.dot_general(a, b, (contract, ((), ())), preferred_element_type=f32)


def copies(pairs, sems):
    return [pltpu.make_async_copy(src, dst, sems.at[i]) for i, (src, dst) in enumerate(pairs)]


def rank_of(routes, experts, toks):
    e = iota((experts, toks), 0)
    first, second = e == routes[0:1, :], e == routes[1:2, :]
    named = first | second
    hot = jnp.where(named, 1.0, 0.0).astype(bf16)
    before = jnp.where(iota((toks, toks), 0) < iota((toks, toks), 1), 1.0, 0.0).astype(bf16)
    return first, second, jnp.where(named, mm(hot, before), -1.0)


def pack_kernel(routes_h, combine_h, tokens_h, grads_h, out_h, routes, combine, tokens, grads, out, last, ins, outs):
    experts = out.shape[0]
    toks, width = tokens.shape
    blocks = width // LANES
    half = blocks * SUB
    arriving = copies(
        [(routes_h, routes), (combine_h, combine), (tokens_h, tokens), (grads_h, grads)], ins
    )
    for c in arriving:
        c.start()
    arriving[0].wait()
    first, second, rank = rank_of(routes, experts, toks)
    slot = iota((experts, SUB, toks), 1)
    spread = jnp.broadcast_to(rank[:, None, :], (experts, SUB, toks))
    pick = jnp.where(spread == slot.astype(f32), 1.0, 0.0)
    pick = pick.reshape(experts * SUB, toks).astype(bf16)
    ninth = jnp.where(rank == float(SUB), 1.0, 0.0).astype(bf16)
    pieces = [slice(at, at + 2 * SUB) for at in range(0, 2 * half + 2 * SUB, 2 * SUB)]
    leaving = copies([(out.at[:, p], out_h.at[:, p]) for p in pieces], outs)
    last[...] = jnp.zeros(last.shape, f32)
    arriving[1].wait()
    prob = combine[...].astype(f32)
    prob = jnp.where(first, prob[0:1, :], jnp.where(second, prob[1:2, :], 0.0))
    lane = iota((experts, LANES), 1)
    row = jnp.zeros((experts, LANES), f32)
    for r in range(CAP):
        value = jnp.sum(jnp.where(rank == float(r), prob, 0.0), axis=1, keepdims=True)
        row = jnp.where(lane == r, value, row)
    place = 2 * blocks
    last[place // SUB, pl.ds(place % SUB, experts, stride=SUB), :] = row
    for i, source in enumerate((tokens, grads)):
        arriving[2 + i].wait()
        rows = mm(pick, source[...])
        for c in range(blocks):
            tile = rows[:, c * LANES : (c + 1) * LANES].reshape(experts, SUB, LANES)
            at = i * half + c * SUB
            out[:, at : at + SUB, :] = tile.astype(bf16)
            if c % 2:
                leaving[(i * blocks + c) // 2].start()
        rows = mm(ninth, source[...])
        for c in range(blocks):
            place = i * blocks + c
            last[place // SUB, pl.ds(place % SUB, experts, stride=SUB), :] = rows[:, c * LANES : (c + 1) * LANES]
    for k in range(2):
        at = 2 * half + k * SUB
        out[:, at : at + SUB, :] = last[k].reshape(experts, SUB, LANES).astype(bf16)
    leaving[-1].start()
    for c in leaving:
        c.wait()


def pack(routes, combine, tokens, grads, experts):
    toks, width = tokens.shape
    shape = (experts, (2 * width // LANES) * SUB + 2 * SUB, LANES)
    args = (routes, combine, tokens, grads)
    return pl.pallas_call(
        pack_kernel,
        in_specs=[pl.BlockSpec(memory_space=pltpu.HBM)] * 4,
        out_specs=pl.BlockSpec(memory_space=pltpu.HBM),
        out_shape=jax.ShapeDtypeStruct(shape, bf16),
        scratch_shapes=[pltpu.VMEM(a.shape, a.dtype) for a in args]
        + [
            pltpu.VMEM(shape, bf16),
            pltpu.VMEM((2, experts * SUB, LANES), f32),
            pltpu.SemaphoreType.DMA((4,)),
            pltpu.SemaphoreType.DMA((width // LANES + 1,)),
        ],
        compiler_params=params(WHOLE),
        name="pack",
    )(*args)


def stage_kernel(gate, up, down, out):
    for i, weight in enumerate((gate, up, down)):
        out[i] = weight[0].astype(f32).T.astype(bf16)


def stage(*weights):
    _, hidden, width = weights[0].shape
    return pl.pallas_call(
        stage_kernel,
        out_shape=jax.ShapeDtypeStruct((len(weights), width, hidden), bf16),
        compiler_params=params(),
        cost_estimate=pl.CostEstimate(
            flops=3 * width * hidden, bytes_accessed=12 * width * hidden, transcendentals=0
        ),
        name="stage",
    )(*weights)


def unpack(recv, rows_x, rows_dy, last):
    experts = recv.shape[0]
    blocks = rows_x.shape[1] // LANES
    main = experts * SUB

    def tile(at):
        return recv[:, at : at + SUB, :].reshape(main, LANES)

    for k in range(2):
        last[k] = tile((2 * blocks + k) * SUB).astype(f32)

    def taken(place):
        return last[place // SUB, pl.ds(place % SUB, experts, stride=SUB), :]

    for i, rows in enumerate((rows_x, rows_dy)):
        for c in range(blocks):
            lanes = slice(c * LANES, (c + 1) * LANES)
            rows[0:main, lanes] = tile((i * blocks + c) * SUB)
            rows[main:, lanes] = taken(i * blocks + c).astype(bf16)
    return taken(2 * blocks)


def project_kernel(me, recv, weights, part, own, probs, rows_x, rows_dy, last):
    groups = part.shape[0]
    _, width, hidden = weights.shape
    main = recv.shape[0] * SUB
    share = main // groups
    probs[...] = unpack(recv, rows_x, rows_dy, last)
    for i, rows in enumerate((rows_x, rows_x, rows_dy)):
        lanes = slice(i * hidden, (i + 1) * hidden)
        value = mm(rows[...], weights[i])
        for j in range(groups):
            piece = jnp.concatenate(
                [value[j * share : (j + 1) * share], value[main + j * SUB : main + (j + 1) * SUB]]
            )
            part[j, :, lanes] = piece.astype(bf16)

            @pl.when(me[0] == j)
            def _(piece=piece, lanes=lanes):
                own[:, lanes] = piece


def unpacked(experts, width):
    rows = pltpu.VMEM((experts * CAP, width), bf16)
    return [rows, rows, pltpu.VMEM((2, experts * SUB, LANES), f32)]


def project(me, recv, weights, groups):
    experts = recv.shape[0]
    _, width, hidden = weights.shape
    total = experts * CAP
    count = total // groups
    vmem = pl.BlockSpec(memory_space=pltpu.VMEM)
    return pl.pallas_call(
        project_kernel,
        in_specs=[pl.BlockSpec(memory_space=pltpu.SMEM)] + [vmem] * 2,
        out_shape=(
            jax.ShapeDtypeStruct((groups, count, 3 * hidden), bf16),
            jax.ShapeDtypeStruct((count, 3 * hidden), f32),
            jax.ShapeDtypeStruct((experts, LANES), f32),
        ),
        scratch_shapes=unpacked(experts, width),
        compiler_params=params(),
        name="project",
    )(me, recv, weights)


def terms_kernel(me, parts, own, probs, out):
    groups, count, _ = parts.shape
    hidden = parts.shape[2] // 3
    main = count - SUB
    near = probs[pl.ds(pl.multiple_of(me[0] * SUB, SUB), SUB), :]
    lane = iota((SUB, SUB, LANES), 2)
    spread = jnp.broadcast_to(near[:, None, :], (SUB, SUB, LANES))
    picked = jnp.sum(jnp.where(lane == iota((SUB, SUB, LANES), 1), spread, 0.0), axis=2, keepdims=True)
    ninth = jnp.sum(jnp.where(iota((SUB, LANES), 1) == SUB, near, 0.0), axis=1, keepdims=True)
    weight = jnp.concatenate([picked.reshape(main, 1), ninth])

    def total(i):
        lanes = slice(i * hidden, (i + 1) * hidden)
        value = own[:, lanes]
        for j in range(groups):
            value = value + jnp.where(me[0] == j, 0.0, parts[j, :, lanes].astype(f32))
        return value

    gate_pre, up_pre, grad_hid = total(0), total(1), total(2)
    sig = jax.nn.sigmoid(gate_pre)
    silu_out = gate_pre * sig
    inner = silu_out * up_pre
    scaled = weight * grad_hid
    rows = (
        scaled * up_pre * (sig * (1.0 + gate_pre * (1.0 - sig))),
        scaled * silu_out,
        weight * inner,
    )
    per = hidden // LANES
    for i in range(3 * per):
        block = rows[i // per][:, i % per * LANES : (i % per + 1) * LANES].astype(bf16)
        for j in range(out.shape[0]):
            out[j, i * count : (i + 1) * count, :] = block
    score = jnp.sum(inner * grad_hid, axis=1, keepdims=True)
    cube = (SUB, SUB, LANES)
    lane = iota(cube, 2)
    direct = jnp.broadcast_to(score[:main].reshape(SUB, SUB, 1), cube)
    table = jnp.sum(jnp.where(lane % TERM == iota(cube, 1), direct, 0.0), axis=1)
    lane = iota((SUB, LANES), 1)
    table = jnp.where(lane % TERM == SUB, score[main:], table)
    high = table.astype(bf16).astype(f32)
    middle = (table - high).astype(bf16).astype(f32)
    low = table - high - middle
    table = jnp.where(lane < TERM, high, jnp.where(lane < 2 * TERM, middle, low))
    for j in range(out.shape[0]):
        out[j, 3 * per * count :, :] = table.astype(bf16)


def terms(me, parts, own, probs, times):
    count, wide = own.shape
    vmem = pl.BlockSpec(memory_space=pltpu.VMEM)
    return pl.pallas_call(
        terms_kernel,
        in_specs=[pl.BlockSpec(memory_space=pltpu.SMEM)] + [vmem] * 3,
        out_shape=jax.ShapeDtypeStruct((times, count * wide // LANES + SUB, LANES), bf16),
        compiler_params=params(),
        name="terms",
    )(me, parts, own, probs)


def outer_kernel(routes, rows, recv, gate, up, down, ranks, rows_x, rows_dy, last):
    groups = rows.shape[0]
    hidden = gate.shape[1]
    per = hidden // LANES
    count = (rows.shape[1] - SUB) // (3 * per)
    main = count - SUB
    unpack(recv, rows_x, rows_dy, last)

    def block(i):
        at = i * count
        direct = rows[:, at : at + main, :].astype(f32).reshape(groups * main, LANES)
        ninth = rows[:, at + main : at + count, :].astype(f32).reshape(groups * SUB, LANES)
        return jnp.concatenate([direct, ninth]).astype(bf16)

    for i, (other, out) in enumerate(((rows_x, gate), (rows_x, up), (rows_dy, down))):
        value = jnp.concatenate([block(i * per + c) for c in range(per)], axis=1)
        out[0] = mm(value, other[...], ((0,), (0,))).astype(bf16)
    first, second, rank = rank_of(routes, recv.shape[0], routes.shape[1])
    for k, mine in enumerate((first, second)):
        ranks[k : k + 1, :] = jnp.sum(jnp.where(mine, rank, 0.0), axis=0, keepdims=True)


def outer(routes, rows, recv, hidden, width):
    experts = recv.shape[0]
    total = experts * CAP
    return pl.pallas_call(
        outer_kernel,
        out_shape=(jax.ShapeDtypeStruct((1, hidden, width), bf16),) * 3
        + (jax.ShapeDtypeStruct(routes.shape, f32),),
        scratch_shapes=unpacked(experts, width),
        compiler_params=params(),
        cost_estimate=pl.CostEstimate(
            flops=6 * total * width * hidden, bytes_accessed=8 * total * width, transcendentals=0
        ),
        name="outer",
    )(routes, rows, recv)


def place_kernel(routes, ranks, scores, out):
    experts, toks = scores.shape[0], routes.shape[1]
    table = scores[:, 0 : 3 * TERM].astype(bf16)
    e = iota((experts, toks), 0)
    slot = (iota((3 * TERM, toks), 0) & (TERM - 1)).astype(f32)
    for k in range(2):
        hot = jnp.where(e == routes[k : k + 1, :], 1.0, 0.0).astype(bf16)
        taken = mm(table, hot, ((0,), (0,)))
        taken = jnp.where(slot == ranks[k : k + 1, :], taken, 0.0)
        out[k : k + 1, :] = jnp.sum(taken, axis=0, keepdims=True)


def place(routes, ranks, scores):
    return pl.pallas_call(
        place_kernel,
        out_shape=jax.ShapeDtypeStruct(routes.shape, f32),
        compiler_params=params(),
        name="place",
    )(routes, ranks, scores)


def local(tokens, grad_out, combine, routes, w_gate, w_up, w_down):
    experts, groups = lax.axis_size("expert"), lax.axis_size("dp")
    hidden = w_gate.shape[1]
    y, core = lax.axis_index("dp").astype(i32), lax.axis_index("expert").astype(i32) & 1
    ends = jnp.where(2 * y < groups, 2 * y, 2 * (groups - y) - 1)
    me = jnp.where(core == 1, lax.rem(TURN + groups - y, groups), ends).reshape(1)
    by_slot = routes.T
    packed = pack(by_slot, combine.T, tokens, grad_out, experts)
    recv = lax.all_to_all(packed, "expert", split_axis=0, concat_axis=0, tiled=True)
    part, own, probs = project(me, recv, stage(w_gate, w_up, w_down), groups)
    orders = (
        [groups - 1 - j // 2 if j % 2 else j // 2 for j in range(groups)],
        [(TURN - j) % groups for j in range(groups)],
    )
    both = ("expert", "dp")
    lines = [[e * groups + place for place in orders[e % 2]] for e in range(experts)]

    def exchange(pieces):
        return lax.all_to_all(
            pieces, both, split_axis=0, concat_axis=0, tiled=True, axis_index_groups=lines
        )

    def by_source(rows):
        return rows, rows[:, -SUB:, :].astype(f32).reshape(experts, 1, LANES)

    def even(part, own, probs):
        return by_source(exchange(terms(me, exchange(part), own, probs, groups)))

    def odd(part, own, probs):
        mine = terms(me, exchange(part), own, probs, 1)
        return by_source(lax.all_gather(mine, both, axis=0, tiled=True, axis_index_groups=lines))

    rows, scores = lax.cond(core == 0, even, odd, part, own, probs)
    returned = lax.all_to_all(scores, "expert", split_axis=0, concat_axis=0, tiled=True)
    *grads, ranks = outer(by_slot, rows, recv, hidden, tokens.shape[1])
    return tuple(grads) + (place(by_slot, ranks, returned.reshape(experts, LANES)).T,)


def solution(mesh):
    placed = (
        P("expert", "dp"),
        P("expert", "dp"),
        P("expert", None),
        P("expert", None),
        P("expert", None, "dp"),
        P("expert", None, "dp"),
        P("expert", None, "dp"),
    )
    return jax.shard_map(
        local,
        mesh=mesh,
        in_specs=placed,
        out_specs=(
            P("expert", None, "dp"),
            P("expert", None, "dp"),
            P("expert", None, "dp"),
            P("expert", None),
        ),
        check_vma=False,
    )
```

```python
import functools

import jax
import jax.numpy as jnp
from jax import lax
from jax.experimental import pallas as pl
from jax.experimental.pallas import tpu as pltpu
from jax.sharding import PartitionSpec as P

bf16, f32, i32 = jnp.bfloat16, jnp.float32, jnp.int32
LANES, SUB = 128, 8
TERM = 16
TURN = 5
CAP = 9
LIMIT = 32 * 2**20
WHOLE = 64 * 2**20 - 2**19


def params(limit=LIMIT):
    return pltpu.CompilerParams(vmem_limit_bytes=limit)


def iota(shape, dim):
    return lax.broadcasted_iota(i32, shape, dim)


def mm(a, b, contract=((1,), (0,))):
    return lax.dot_general(a, b, (contract, ((), ())), preferred_element_type=f32)


def copies(pairs, sems):
    return [pltpu.make_async_copy(src, dst, sems.at[i]) for i, (src, dst) in enumerate(pairs)]


def rank_of(routes, experts, toks):
    e = iota((experts, toks), 0)
    first, second = e == routes[0:1, :], e == routes[1:2, :]
    named = first | second
    hot = jnp.where(named, 1.0, 0.0).astype(bf16)
    before = jnp.where(iota((toks, toks), 0) < iota((toks, toks), 1), 1.0, 0.0).astype(bf16)
    return first, second, jnp.where(named, mm(hot, before), -1.0)


def pack_kernel(routes_h, combine_h, tokens_h, grads_h, out_h, routes, combine, tokens, grads, out, last, ins, outs):
    experts = out.shape[0]
    toks, width = tokens.shape
    blocks = width // LANES
    half = blocks * SUB
    arriving = copies(
        [(routes_h, routes), (combine_h, combine), (tokens_h, tokens), (grads_h, grads)], ins
    )
    for c in arriving:
        c.start()
    arriving[0].wait()
    first, second, rank = rank_of(routes, experts, toks)
    slot = iota((experts, SUB, toks), 1)
    spread = jnp.broadcast_to(rank[:, None, :], (experts, SUB, toks))
    pick = jnp.where(spread == slot.astype(f32), 1.0, 0.0)
    pick = pick.reshape(experts * SUB, toks).astype(bf16)
    ninth = jnp.where(rank == float(SUB), 1.0, 0.0).astype(bf16)
    pieces = [slice(at, at + 2 * SUB) for at in range(0, 2 * half + 2 * SUB, 2 * SUB)]
    leaving = copies([(out.at[:, p], out_h.at[:, p]) for p in pieces], outs)
    last[...] = jnp.zeros(last.shape, f32)
    arriving[1].wait()
    prob = combine[...].astype(f32)
    prob = jnp.where(first, prob[0:1, :], jnp.where(second, prob[1:2, :], 0.0))
    lane = iota((experts, LANES), 1)
    row = jnp.zeros((experts, LANES), f32)
    for r in range(CAP):
        value = jnp.sum(jnp.where(rank == float(r), prob, 0.0), axis=1, keepdims=True)
        row = jnp.where(lane == r, value, row)
    place = 2 * blocks
    last[place // SUB, pl.ds(place % SUB, experts, stride=SUB), :] = row
    for i, source in enumerate((tokens, grads)):
        arriving[2 + i].wait()
        rows = mm(pick, source[...])
        for c in range(blocks):
            tile = rows[:, c * LANES : (c + 1) * LANES].reshape(experts, SUB, LANES)
            at = i * half + c * SUB
            out[:, at : at + SUB, :] = tile.astype(bf16)
            if c % 2:
                leaving[(i * blocks + c) // 2].start()
        rows = mm(ninth, source[...])
        for c in range(blocks):
            place = i * blocks + c
            last[place // SUB, pl.ds(place % SUB, experts, stride=SUB), :] = rows[:, c * LANES : (c + 1) * LANES]
    for k in range(2):
        at = 2 * half + k * SUB
        out[:, at : at + SUB, :] = last[k].reshape(experts, SUB, LANES).astype(bf16)
    leaving[-1].start()
    for c in leaving:
        c.wait()


def pack(routes, combine, tokens, grads, experts):
    toks, width = tokens.shape
    shape = (experts, (2 * width // LANES) * SUB + 2 * SUB, LANES)
    args = (routes, combine, tokens, grads)
    return pl.pallas_call(
        pack_kernel,
        in_specs=[pl.BlockSpec(memory_space=pltpu.HBM)] * 4,
        out_specs=pl.BlockSpec(memory_space=pltpu.HBM),
        out_shape=jax.ShapeDtypeStruct(shape, bf16),
        scratch_shapes=[pltpu.VMEM(a.shape, a.dtype) for a in args]
        + [
            pltpu.VMEM(shape, bf16),
            pltpu.VMEM((2, experts * SUB, LANES), f32),
            pltpu.SemaphoreType.DMA((4,)),
            pltpu.SemaphoreType.DMA((width // LANES + 1,)),
        ],
        compiler_params=params(WHOLE),
        name="pack",
    )(*args)


def stage_kernel(gate, up, down, out):
    for i, weight in enumerate((gate, up, down)):
        hidden = weight.shape[1]
        out[:, i * hidden : (i + 1) * hidden] = weight[0].astype(f32).T.astype(bf16)


def stage(*weights):
    _, hidden, width = weights[0].shape
    return pl.pallas_call(
        stage_kernel,
        out_shape=jax.ShapeDtypeStruct((width, len(weights) * hidden), bf16),
        compiler_params=params(),
        cost_estimate=pl.CostEstimate(
            flops=3 * width * hidden, bytes_accessed=12 * width * hidden, transcendentals=0
        ),
        name="stage",
    )(*weights)


def unpack(recv, rows_x, rows_dy, last):
    experts = recv.shape[0]
    blocks = rows_x.shape[1] // LANES
    main = experts * SUB

    def tile(at):
        return recv[:, at : at + SUB, :].reshape(main, LANES)

    for k in range(2):
        last[k] = tile((2 * blocks + k) * SUB).astype(f32)

    def taken(place):
        return last[place // SUB, pl.ds(place % SUB, experts, stride=SUB), :]

    for i, rows in enumerate((rows_x, rows_dy)):
        for c in range(blocks):
            lanes = slice(c * LANES, (c + 1) * LANES)
            rows[0:main, lanes] = tile((i * blocks + c) * SUB)
            rows[main:, lanes] = taken(i * blocks + c).astype(bf16)
    return taken(2 * blocks)


def project_kernel(me, recv, weights, part, own, probs, rows_x, rows_dy, last):
    groups = part.shape[0]
    hidden = weights.shape[1] // 3
    main = recv.shape[0] * SUB
    share = main // groups
    probs[...] = unpack(recv, rows_x, rows_dy, last)
    for rows, lanes in ((rows_x, slice(0, 2 * hidden)), (rows_dy, slice(2 * hidden, 3 * hidden))):
        value = mm(rows[...], weights[:, lanes])
        for j in range(groups):
            piece = jnp.concatenate(
                [value[j * share : (j + 1) * share], value[main + j * SUB : main + (j + 1) * SUB]]
            )
            part[j, :, lanes] = piece.astype(bf16)

            @pl.when(me[0] == j)
            def _(piece=piece, lanes=lanes):
                own[:, lanes] = piece


def unpacked(experts, width):
    rows = pltpu.VMEM((experts * CAP, width), bf16)
    return [rows, rows, pltpu.VMEM((2, experts * SUB, LANES), f32)]


def project(me, recv, weights, groups):
    experts = recv.shape[0]
    width, hidden = weights.shape[0], weights.shape[1] // 3
    total = experts * CAP
    count = total // groups
    vmem = pl.BlockSpec(memory_space=pltpu.VMEM)
    return pl.pallas_call(
        project_kernel,
        in_specs=[pl.BlockSpec(memory_space=pltpu.SMEM)] + [vmem] * 2,
        out_shape=(
            jax.ShapeDtypeStruct((groups, count, 3 * hidden), bf16),
            jax.ShapeDtypeStruct((count, 3 * hidden), f32),
            jax.ShapeDtypeStruct((experts, LANES), f32),
        ),
        scratch_shapes=unpacked(experts, width),
        compiler_params=params(),
        name="project",
    )(me, recv, weights)


def terms_kernel(me, parts, own, probs, out):
    groups, count, _ = parts.shape
    hidden = parts.shape[2] // 3
    main = count - SUB
    near = probs[pl.ds(pl.multiple_of(me[0] * SUB, SUB), SUB), :]
    lane = iota((SUB, SUB, LANES), 2)
    spread = jnp.broadcast_to(near[:, None, :], (SUB, SUB, LANES))
    picked = jnp.sum(jnp.where(lane == iota((SUB, SUB, LANES), 1), spread, 0.0), axis=2, keepdims=True)
    ninth = jnp.sum(jnp.where(iota((SUB, LANES), 1) == SUB, near, 0.0), axis=1, keepdims=True)
    weight = jnp.concatenate([picked.reshape(main, 1), ninth])

    def total(i):
        lanes = slice(i * hidden, (i + 1) * hidden)
        value = own[:, lanes]
        for j in range(groups):
            value = value + jnp.where(me[0] == j, 0.0, parts[j, :, lanes].astype(f32))
        return value

    gate_pre, up_pre, grad_hid = total(0), total(1), total(2)
    sig = jax.nn.sigmoid(gate_pre)
    silu_out = gate_pre * sig
    inner = silu_out * up_pre
    scaled = weight * grad_hid
    rows = (
        scaled * up_pre * (sig * (1.0 + gate_pre * (1.0 - sig))),
        scaled * silu_out,
        weight * inner,
    )
    per = hidden // LANES
    for i in range(3 * per):
        block = rows[i // per][:, i % per * LANES : (i % per + 1) * LANES].astype(bf16)
        for j in range(out.shape[0]):
            out[j, i * count : (i + 1) * count, :] = block
    score = jnp.sum(inner * grad_hid, axis=1, keepdims=True)
    cube = (SUB, SUB, LANES)
    lane = iota(cube, 2)
    direct = jnp.broadcast_to(score[:main].reshape(SUB, SUB, 1), cube)
    table = jnp.sum(jnp.where(lane % TERM == iota(cube, 1), direct, 0.0), axis=1)
    lane = iota((SUB, LANES), 1)
    table = jnp.where(lane % TERM == SUB, score[main:], table)
    high = table.astype(bf16).astype(f32)
    middle = (table - high).astype(bf16).astype(f32)
    low = table - high - middle
    table = jnp.where(lane < TERM, high, jnp.where(lane < 2 * TERM, middle, low))
    for j in range(out.shape[0]):
        out[j, 3 * per * count :, :] = table.astype(bf16)


def terms(me, parts, own, probs, times):
    count, wide = own.shape
    vmem = pl.BlockSpec(memory_space=pltpu.VMEM)
    return pl.pallas_call(
        terms_kernel,
        in_specs=[pl.BlockSpec(memory_space=pltpu.SMEM)] + [vmem] * 3,
        out_shape=jax.ShapeDtypeStruct((times, count * wide // LANES + SUB, LANES), bf16),
        compiler_params=params(),
        name="terms",
    )(me, parts, own, probs)


def outer_kernel(routes, rows, recv, gate, up, down, ranks, rows_x, rows_dy, last):
    groups = rows.shape[0]
    hidden = gate.shape[1]
    per = hidden // LANES
    count = (rows.shape[1] - SUB) // (3 * per)
    main = count - SUB
    unpack(recv, rows_x, rows_dy, last)

    def block(i):
        at = i * count
        direct = rows[:, at : at + main, :].astype(f32).reshape(groups * main, LANES)
        ninth = rows[:, at + main : at + count, :].astype(f32).reshape(groups * SUB, LANES)
        return jnp.concatenate([direct, ninth]).astype(bf16)

    for i, (other, out) in enumerate(((rows_x, gate), (rows_x, up), (rows_dy, down))):
        value = jnp.concatenate([block(i * per + c) for c in range(per)], axis=1)
        out[0] = mm(value, other[...], ((0,), (0,))).astype(bf16)
    first, second, rank = rank_of(routes, recv.shape[0], routes.shape[1])
    for k, mine in enumerate((first, second)):
        ranks[k : k + 1, :] = jnp.sum(jnp.where(mine, rank, 0.0), axis=0, keepdims=True)


def outer(routes, rows, recv, hidden, width):
    experts = recv.shape[0]
    total = experts * CAP
    return pl.pallas_call(
        outer_kernel,
        out_shape=(jax.ShapeDtypeStruct((1, hidden, width), bf16),) * 3
        + (jax.ShapeDtypeStruct(routes.shape, f32),),
        scratch_shapes=unpacked(experts, width),
        compiler_params=params(),
        cost_estimate=pl.CostEstimate(
            flops=6 * total * width * hidden, bytes_accessed=8 * total * width, transcendentals=0
        ),
        name="outer",
    )(routes, rows, recv)


def place_kernel(routes, ranks, scores, out):
    experts, toks = scores.shape[0], routes.shape[1]
    table = scores[:, 0 : 3 * TERM].astype(bf16)
    e = iota((experts, toks), 0)
    slot = (iota((3 * TERM, toks), 0) & (TERM - 1)).astype(f32)
    for k in range(2):
        hot = jnp.where(e == routes[k : k + 1, :], 1.0, 0.0).astype(bf16)
        taken = mm(table, hot, ((0,), (0,)))
        taken = jnp.where(slot == ranks[k : k + 1, :], taken, 0.0)
        out[k : k + 1, :] = jnp.sum(taken, axis=0, keepdims=True)


def place(routes, ranks, scores):
    return pl.pallas_call(
        place_kernel,
        out_shape=jax.ShapeDtypeStruct(routes.shape, f32),
        compiler_params=params(),
        name="place",
    )(routes, ranks, scores)


def local(tokens, grad_out, combine, routes, w_gate, w_up, w_down):
    experts, groups = lax.axis_size("expert"), lax.axis_size("dp")
    hidden = w_gate.shape[1]
    y, core = lax.axis_index("dp").astype(i32), lax.axis_index("expert").astype(i32) & 1
    me = jnp.where(core == 1, lax.rem(TURN + groups - y, groups), y).reshape(1)
    by_slot = routes.T
    packed = pack(by_slot, combine.T, tokens, grad_out, experts)
    recv = lax.all_to_all(packed, "expert", split_axis=0, concat_axis=0, tiled=True)
    part, own, probs = project(me, recv, stage(w_gate, w_up, w_down), groups)
    both = ("expert", "dp")
    lines = [
        [e * groups + ((TURN - j) % groups if e % 2 else j) for j in range(groups)] for e in range(experts)
    ]

    def exchange(pieces):
        return lax.all_to_all(
            pieces, both, split_axis=0, concat_axis=0, tiled=True, axis_index_groups=lines
        )

    def by_source(rows):
        return rows, rows[:, -SUB:, :].astype(f32).reshape(experts, 1, LANES)

    def even(part, own, probs):
        return by_source(exchange(terms(me, exchange(part), own, probs, groups)))

    def odd(part, own, probs):
        mine = terms(me, exchange(part), own, probs, 1)
        return by_source(lax.all_gather(mine, both, axis=0, tiled=True, axis_index_groups=lines))

    rows, scores = lax.cond(core == 0, even, odd, part, own, probs)
    returned = lax.all_to_all(scores, "expert", split_axis=0, concat_axis=0, tiled=True)
    *grads, ranks = outer(by_slot, rows, recv, hidden, tokens.shape[1])
    return tuple(grads) + (place(by_slot, ranks, returned.reshape(experts, LANES)).T,)


def solution(mesh):
    placed = (
        P("expert", "dp"),
        P("expert", "dp"),
        P("expert", None),
        P("expert", None),
        P("expert", None, "dp"),
        P("expert", None, "dp"),
        P("expert", None, "dp"),
    )
    return jax.shard_map(
        local,
        mesh=mesh,
        in_specs=placed,
        out_specs=(
            P("expert", None, "dp"),
            P("expert", None, "dp"),
            P("expert", None, "dp"),
            P("expert", None),
        ),
        check_vma=False,
    )
```
